32 devices in a mesh: st: 8 (over z, x), ch: 4 (over y, core).
Axes of the slice: x: 2, y: 2, z: 4, core: 2. Of those that a mesh axis runs over, the one named last changes fastest.
Arguments:
- waveform: bfloat16 [256, 3, 8704], P('st'), may hold values from -500 to 500
- templates: bfloat16 [416, 32, 512], P('st', 'ch'), may hold values from -50 to 50
- block_of: int32 [4, 416, 2], P('ch'), may hold values from 0 to 7, all different within a row; in each aligned block of 52 rows (0 to 51, 52 to 103, ..., all dimensions but the last counted through in order) at most 17 rows name the same one
- trace_of: int32 [4, 8, 8, 4], P('ch'), may hold values from 0 to 95
Outputs:
- detection: float32 [416, 8192], P('st', 'ch')
The draws below stay inside these ranges and needn't reach their ends.
Inputs may be any that keep to these rules, and one draw needn't show every extreme that they name: `block_of`: a row names two different station blocks; among the 52 templates of one owner (aligned blocks of the template dimension) in one group, no station block is named by more than 17 templates, and some station block is named by exactly 17.
All inputs are finite; a program needn't handle non-finite values.
Results may differ from the reference program's by a relative error of at most 0.00035.
Values may be sent and summed in bfloat16 or wider, within the bound.
A program may use at most 192 MiB of HBM per device.

```python
import math
import jax
import jax.numpy as jnp
import numpy as np
from jax import lax

CHANS = 32
TAPS = 512
K_DEV = 52
S_DEV = 32
CH_DEV = 8
HALF = 4
GROUPS = 4
BLOCKS = 8
OWNERS = 8
TEMPLATES = 416
STATIONS = 256
LAGS = 8192
WIN = 8704
SLOTS = 17


def draw_waveform(key, part):
    key_base, key_trace, key_block = jax.random.split(jax.random.fold_in(key, 11), 3)
    full_shape = (STATIONS, 3, WIN)
    pieces = (WIN + 31) // 32
    noise_base = jax.random.truncated_normal(key_base, -5.0, 5.0, full_shape, jnp.float32)
    log_range = jnp.log(10.0)
    trace_scale = jnp.exp(jax.random.uniform(key_trace, (STATIONS, 3, 1), jnp.float32, 0.0, 1.0) * log_range)
    block_scale = jnp.exp(jax.random.uniform(key_block, (STATIONS, 3, pieces), jnp.float32, 0.0, 1.0) * log_range)
    envelope = jnp.repeat(block_scale, 32, axis=2)[:, :, :WIN]
    return (noise_base * trace_scale * envelope).astype(jnp.bfloat16)


def draw_templates(key, part):
    key_base, key_scale = jax.random.split(jax.random.fold_in(key, 23), 2)
    full_shape = (TEMPLATES, CHANS, TAPS)
    noise_base = jax.random.truncated_normal(key_base, -5.0, 5.0, full_shape, jnp.float32)
    log_range = jnp.log(10.0)
    channel_scale = jnp.exp(jax.random.uniform(key_scale, (TEMPLATES, CHANS, 1), jnp.float32, 0.0, 1.0) * log_range)
    return (noise_base * channel_scale).astype(jnp.bfloat16)


def touch_ends(drawn, rng, least, largest):
    longest = drawn.shape.index(max(drawn.shape))
    spots = []
    for shift in (0, 1):
        where = [jax.random.randint(jax.random.fold_in(rng, axis), (), 0, length) for axis, length in enumerate(drawn.shape)]
        where[longest] = (where[longest] + shift) % drawn.shape[longest]
        spots.append(tuple(where))
    return drawn.at[spots[0]].set(least).at[spots[1]].set(largest)


def deal_out(stream_key, own, number, rows, amount, top, limit, skew):
    order = jax.random.permutation(stream_key, amount)
    packed, usual = shares(amount, rows * top, limit, skew, True), shares(amount, rows * top, limit, skew, False)
    places = jnp.arange(amount)

    def named(lengths, rotation):
        used = int((lengths > 0).sum())
        fixed = max(1, used // 4)
        passed = fixed + (places - fixed + rotation * (used - fixed)) % max(1, amount - fixed)
        return jnp.zeros((amount,), jnp.int32).at[order[jnp.where(places < fixed, places, passed)]].set(jnp.asarray(lengths, jnp.int32))

    lengths = jnp.where(number % 4 == 0, named(packed, number // 4), named(usual, number - number // 4 - 1))
    mixed = jax.random.permutation(jax.random.fold_in(own, 3), amount)
    donor, taker = mixed[0:amount // 2 * 2:2], mixed[1:amount // 2 * 2:2]
    slack = jnp.minimum(lengths[donor] - 1, limit - lengths[taker]) // 2
    slack = jnp.where((donor == order[0]) | (taker == order[0]) | (lengths[taker] == 0), 0, jnp.maximum(slack, 0))
    passed = jax.random.randint(jax.random.fold_in(own, 4), (amount // 2,), 0, 1 << 20) % (slack + 1)
    lengths = lengths.at[donor].add(-passed).at[taker].add(passed)
    items = jnp.searchsorted(jnp.cumsum(lengths), jnp.arange(rows * top), side="right").astype(jnp.int32)
    grid = items.reshape(top, rows).T
    grid = grid[jax.random.permutation(jax.random.fold_in(own, 1), rows)]
    rotation = jax.random.randint(jax.random.fold_in(own, 2), (rows, 1), 0, top)
    return jnp.take_along_axis(grid, (jnp.arange(top)[None, :] + rotation) % top, axis=1)


def shares(number_of, total, bound, slope, full):
    weights = [(1 << 20) // math.isqrt(grade ** slope) + 1 for grade in range(1, number_of + 1)]
    largest = bound if full else min(bound, max(-(-total // number_of), total * weights[0] // sum(weights)))
    least = 1 if total - largest >= number_of - 1 else 0
    given, rest = [largest] + [least] * (number_of - 1), total - largest - least * (number_of - 1)
    while rest > 0:
        free = [i for i in range(1, number_of) if given[i] < largest] or [i for i in range(1, number_of) if given[i] < bound]
        pool, budget = sum([weights[i] for i in free]), rest
        for i in free:
            more = min(bound - given[i], max(1, budget * weights[i] // pool), rest)
            given[i] = given[i] + more
            rest = rest - more
    return np.array(given)


def setup_inputs(seed: int = 0) -> dict:
    arg_keys = jax.random.split(jax.random.key(seed), 5)
    waveform = draw_waveform(jax.random.fold_in(arg_keys[4], 71), 0)
    templates = draw_templates(jax.random.fold_in(arg_keys[4], 71), 0)
    block_of_keys = jax.random.split(jax.random.fold_in(arg_keys[2], 1), GROUPS * TEMPLATES // K_DEV)
    block_of_turns = jax.random.permutation(jax.random.fold_in(arg_keys[2], 3), GROUPS * TEMPLATES // K_DEV)
    block_of = jax.vmap(lambda own, number: deal_out(jax.random.fold_in(arg_keys[2], 2), own, number, K_DEV, BLOCKS, 2, SLOTS, 2))(block_of_keys, block_of_turns).reshape((GROUPS, TEMPLATES, 2))
    trace_of = touch_ends(jax.random.randint(arg_keys[3], (GROUPS, OWNERS, BLOCKS, HALF), 0, 3 * S_DEV), jax.random.fold_in(arg_keys[3], 1), 0, (3 * S_DEV) - 1).astype(jnp.int32)
    return {"waveform": waveform, "templates": templates, "block_of": block_of, "trace_of": trace_of}


EPSILON = 1e-05

def reference(waveform, templates, block_of, trace_of):
    rows_all = waveform.reshape(STATIONS * 3, WIN)
    halves = (jnp.arange(CH_DEV) // HALF).astype(jnp.int32)
    chosen_blocks = jnp.take(block_of, halves, axis=2).astype(jnp.int32)
    group_ids = jnp.arange(GROUPS, dtype=jnp.int32)[:, None, None]
    owner_ids = (jnp.arange(TEMPLATES, dtype=jnp.int32) // K_DEV)[None, :, None]
    chan_pos = (jnp.arange(CH_DEV, dtype=jnp.int32) % HALF)[None, None, :]
    picks = trace_of[group_ids, owner_ids, chosen_blocks, chan_pos]
    row_index = (chosen_blocks * (3 * S_DEV) + picks).astype(jnp.int32)
    row_index = jnp.transpose(row_index, (1, 0, 2)).reshape(TEMPLATES, CHANS)
    fft_len = 2 ** (WIN + TAPS).bit_length()
    group_size = math.gcd(TEMPLATES, 32)

    def group_terms(operands):
        index_block, filter_block = operands
        traces = jnp.take(rows_all, index_block, axis=0).astype(jnp.float32)
        filters = filter_block.astype(jnp.float32)
        spectrum = jnp.fft.rfft(traces, fft_len, axis=-1) * jnp.conj(jnp.fft.rfft(filters, fft_len, axis=-1))
        raw_sum = jnp.fft.irfft(spectrum, fft_len, axis=-1)[..., :LAGS]
        energy = lax.reduce_window(traces * traces, jnp.array(0, traces.dtype), lax.add, (1, 1, TAPS), (1, 1, 1), 'VALID')[..., :LAGS]
        filter_power = lax.optimization_barrier(jnp.mean(filters * filters, axis=-1, keepdims=True))
        coherence = raw_sum / (TAPS * jnp.sqrt((energy / TAPS + EPSILON) * (filter_power + EPSILON)))
        return lax.optimization_barrier(jnp.sum(coherence, axis=1))
    result = lax.map(group_terms, (row_index.reshape(-1, group_size, CHANS), templates.reshape(-1, group_size, CHANS, TAPS)))
    return result.reshape(TEMPLATES, LAGS)
```

```python
import functools

import jax
import jax.numpy as jnp
import numpy as np
from jax import lax
from jax.experimental import pallas as pl
from jax.experimental.pallas import tpu as pltpu
from jax.sharding import PartitionSpec as P

EPSILON = 1e-05
SHIFTS = 16
LANES = 128
TURNS = LANES // SHIFTS
STEP = 4
MESH = pl.DeviceIdType.MESH
F32 = jnp.float32
BF16 = jnp.bfloat16


def flipped(me, i, size):
    out, k = 0, 1
    while k < size:
        out = out + k * lax.rem(lax.div(me, k) + lax.div(i, k), 2)
        k *= 2
    return out


def kernel(
    dims,
    order_ref,
    place_ref,
    select_ref,
    wave_ref,
    filters_ref,
    steps_ref,
    out_ref,
    stage,
    send,
    recv,
    skew,
    gains,
    plain,
    rolled,
    suffix,
    before,
    total,
    right,
    scale,
    parts,
    turned,
    near_recv,
    far_send,
    far_recv,
    summed,
    send_sem,
    recv_sem,
    near_send_sem,
    near_recv_sem,
    far_send_sem,
    far_recv_sem,
):
    blocks, slots, templates, half, taps, used, depth, lags, chunk, lag = dims
    me = lax.axis_index("st")
    mine = lax.axis_index("ch")
    near, far = flipped(mine, 1, 4), flipped(mine, 2, 4)
    rows = half * used

    barrier = pltpu.get_barrier_semaphore()

    def greet(i, carry):
        pl.semaphore_signal(
            barrier, inc=1, device_id={"st": flipped(me, i, blocks)}, device_id_type=MESH
        )
        return carry

    lax.fori_loop(1, blocks, greet, 0)
    for other in (near, far):
        pl.semaphore_signal(barrier, inc=1, device_id={"ch": other}, device_id_type=MESH)

    wide = 4 * LANES

    def gather(i, carry):
        at = pl.ds(pl.multiple_of(i * wide, wide), wide)
        tile = jnp.dot(select_ref[...], wave_ref[:, at], preferred_element_type=F32)
        for j in range(4):
            spots = pl.ds(i * 4 + j, blocks * half, stride=used)
            stage[spots, :] = tile[:, j * LANES : (j + 1) * LANES]
        return carry

    lax.fori_loop(0, used * LANES // wide, gather, 0)

    def staged(block):
        return stage[pl.ds(pl.multiple_of(block * rows, 16), rows), :].astype(BF16)

    pl.semaphore_wait(barrier, blocks + 1)

    def trace_copy(i):
        other = flipped(me, i, blocks)
        return pltpu.make_async_remote_copy(
            src_ref=send.at[other],
            dst_ref=recv.at[me],
            send_sem=send_sem.at[i],
            recv_sem=recv_sem.at[i],
            device_id={"st": other},
            device_id_type=MESH,
        )

    def post(i, carry):
        other = flipped(me, i, blocks)
        send[other] = staged(other)
        trace_copy(i).start()
        return carry

    lax.fori_loop(1, blocks, post, 0)
    recv[me] = staged(me)

    def spread(k, carry):
        taken = filters_ref[k].astype(F32)
        mean = jnp.sum(taken * taken, axis=1, keepdims=True) / taps
        gain = 1.0 / (taps * jnp.sqrt(mean + EPSILON))
        gain = jnp.broadcast_to(gain, (2 * half, LANES))
        longer = jnp.concatenate([taken, jnp.zeros((2 * half, depth - taps), F32)], axis=1)
        for c in range(2 * half):
            wave = jnp.broadcast_to(longer[c : c + 1], (SHIFTS, depth))
            wave = pltpu.roll(wave, 0, 1, stride=1, stride_axis=0)
            skew[2 * k + c // half, c % half] = wave.astype(BF16)
        gains[2 * k] = gain[:half]
        gains[2 * k + 1] = gain[half:]
        return carry

    lax.fori_loop(0, templates, spread, 0)

    lane = lax.broadcasted_iota(jnp.int32, (SHIFTS, LANES), 1)
    low = lane < LANES // 2
    plain[rows:, :] = jnp.zeros((8, LANES), F32)
    rolled[:, rows:, :] = jnp.zeros((TURNS - 1, 8, LANES), F32)
    extra = depth // LANES

    def prepare(source):
        x = recv[source].astype(F32)
        plain[:rows, :] = x
        squares = x * x
        high = squares.astype(BF16)
        rest = (squares - high.astype(F32)).astype(BF16)
        sums = jnp.dot(
            jnp.concatenate([high, rest], axis=1), steps_ref[...], preferred_element_type=F32
        )
        suffix[:rows, :] = sums[:, :LANES]
        before[:rows, :] = sums[:, LANES : 2 * LANES]
        total[:rows, :] = sums[:, 2 * LANES :]
        for m in range(1, TURNS):
            rolled[m - 1, :rows, :] = pltpu.roll(x, LANES - SHIFTS * m, 1)
        for c in range(half):
            for m in range(TURNS):
                held = plain if m == 0 else rolled.at[m - 1]
                found = [
                    held[pl.ds(c * used + b, SHIFTS, stride=STEP), :]
                    for b in range(STEP + extra - (m == 0))
                ]
                for b in range(STEP + extra - 1):
                    tile = found[b]
                    if m > 0:
                        tile = jnp.where(lane < LANES - SHIFTS * m, tile, found[b + 1])
                    right[c, m * TURNS + b] = tile.astype(BF16)
        for c in range(0, half, 2):
            roots = []
            for d in (c, c + 1):
                for b in range(STEP):
                    base = d * used + b
                    energy = suffix[pl.ds(base, SHIFTS, stride=STEP), :]
                    for q in range(1, taps // LANES):
                        energy = energy + total[pl.ds(base + q, SHIFTS, stride=STEP), :]
                    energy = energy + before[pl.ds(base + taps // LANES, SHIFTS, stride=STEP), :]
                    roots.append(lax.rsqrt(energy / taps + EPSILON))
            roots = jnp.concatenate(roots, axis=0).T
            for t in range(TURNS // 2):
                even = roots[2 * t * SHIFTS : (2 * t + 1) * SHIFTS]
                odd = roots[(2 * t + 1) * SHIFTS : (2 * t + 2) * SHIFTS]
                at = slice(t * LANES, (t + 1) * LANES)
                scale[c, :, at] = jnp.where(low, even, pltpu.roll(odd, LANES // 2, 1))
                scale[c + 1, :, at] = jnp.where(low, pltpu.roll(even, LANES // 2, 1), odd)

    def products(source):
        base = source * slots
        for c in range(half):
            left = jnp.concatenate([skew[order_ref[base + g], c] for g in range(slots)], axis=0)
            tiles = []
            for m in range(TURNS):
                for b in range(STEP):
                    tiles.append(
                        jnp.concatenate(
                            [right[c, m * TURNS + b + q] for q in range(extra)], axis=1
                        )
                    )
            raw = lax.dot_general(
                left,
                jnp.concatenate(tiles, axis=0),
                (((1,), (1,)), ((), ())),
                preferred_element_type=F32,
            )
            for g in range(slots):
                gain = gains[order_ref[base + g], pl.ds(c, 1), :]
                gain = jnp.concatenate([gain] * (lags // SHIFTS // LANES), axis=1)
                term = raw[g * SHIFTS : (g + 1) * SHIFTS] * (scale[c] * gain)
                if c == 0:
                    parts[base + g] = term
                else:
                    parts[base + g] += term

    def work(i, carry):
        source = flipped(me, i, blocks)

        @pl.when(i > 0)
        def _():
            trace_copy(i).wait_recv()

        prepare(source)
        products(source)
        return carry

    lax.fori_loop(0, blocks, work, 0)

    piece = lags // LANES // 4
    chunks = templates // chunk

    def some(j):
        return pl.ds(j * chunk, chunk)

    def spots(number):
        return pl.ds(pl.multiple_of(number * piece, 8), piece)

    def near_copy(j, side):
        number = lax.rem(near, 2) + 2 * side
        return pltpu.make_async_remote_copy(
            src_ref=turned.at[some(j), spots(number)],
            dst_ref=near_recv.at[side, some(j)],
            send_sem=near_send_sem.at[j, side],
            recv_sem=near_recv_sem.at[j, side],
            device_id={"ch": near},
            device_id_type=MESH,
        )

    def far_copy(j):
        return pltpu.make_async_remote_copy(
            src_ref=far_send.at[some(j)],
            dst_ref=far_recv.at[some(j)],
            send_sem=far_send_sem.at[j],
            recv_sem=far_recv_sem.at[j],
            device_id={"ch": far},
            device_id_type=MESH,
        )

    own_side, far_side = lax.div(mine, 2), lax.div(far, 2)

    def turn(j):
        for pair in range(chunk // 2):
            first = j * chunk + 2 * pair
            both = [
                parts[place_ref[2 * k]] + parts[place_ref[2 * k + 1]] for k in (first, first + 1)
            ]
            stack = []
            for t in range(TURNS // 2):
                a, b = (x[:, t * LANES : (t + 1) * LANES] for x in both)
                stack.append(jnp.where(low, a, pltpu.roll(b, LANES // 2, 1)))
                stack.append(jnp.where(low, pltpu.roll(a, LANES // 2, 1), b))
            flat = jnp.concatenate(stack, axis=0).T
            for i in range(2):
                for b in range(STEP):
                    at = (i * STEP + b) * SHIFTS
                    turned[first + i, pl.ds(b, SHIFTS, stride=STEP), :] = flat[at : at + SHIFTS]

    def pass_on(j):
        near_copy(j, far_side).wait_recv()
        far_send[some(j)] = turned[some(j), spots(far)] + near_recv[far_side, some(j)]
        far_copy(j).start()

    def reduce(j, carry):
        turn(j)
        near_copy(j, far_side).start()
        near_copy(j, own_side).start()

        @pl.when(j >= lag)
        def _():
            pass_on(j - lag)

        return carry

    lax.fori_loop(0, chunks, reduce, 0)

    def drain(j, carry):
        pass_on(j)
        return carry

    lax.fori_loop(chunks - lag, chunks, drain, 0)

    def finish(j, carry):
        near_copy(j, own_side).wait_recv()
        far_copy(j).wait_recv()
        value = turned[some(j), spots(mine)] + near_recv[own_side, some(j)] + far_recv[some(j)]
        out_ref[some(j)] = value
        near_copy(j, far_side).wait_send()
        near_copy(j, own_side).wait_send()
        far_copy(j).wait_send()
        return carry

    lax.fori_loop(0, chunks, finish, 0)

    def close(i, carry):
        trace_copy(i).wait_send()
        return carry

    lax.fori_loop(1, blocks, close, 0)


def per_device(waveform, templates, block_of, trace_of):
    me = lax.axis_index("st")
    blocks = lax.axis_size("st")
    own, chans, taps = templates.shape
    half = chans // 2
    stations, comps, window = waveform.shape
    lags = window - taps
    used = window // LANES
    depth = taps + LANES
    pairs = 2 * own
    slots = -(-13 * pairs // (10 * blocks))
    chunk = 4
    assert own % chunk == 0 and lags == 64 * LANES and used % 4 == 0

    sources = lax.dynamic_index_in_dim(block_of[0].reshape(blocks, own, 2), me, 0, keepdims=False)
    named = sources.reshape(pairs)
    ids = jnp.arange(pairs, dtype=jnp.int32)
    earlier = (named[None, :] == named[:, None]) & (ids[None, :] < ids[:, None])
    place = named * slots + jnp.sum(earlier.astype(jnp.int32), axis=1)
    where = jnp.arange(blocks * slots, dtype=jnp.int32)
    order = jnp.sum(jnp.where(place[None, :] == where[:, None], ids[None, :], 0), axis=1)

    wanted = lax.dynamic_index_in_dim(trace_of[0], me, 1, keepdims=False).reshape(-1)
    rows = jnp.arange(stations * comps, dtype=jnp.int32)
    trace = (rows % stations) * comps + rows // stations
    select = (wanted[:, None] == trace[None, :]).astype(BF16)
    wave = jnp.transpose(waveform, (1, 0, 2)).reshape(stations * comps, window)

    spots = np.arange(LANES)
    later = spots[:, None] >= spots[None, :]
    steps = np.concatenate([later, ~later, np.ones_like(later)], axis=1)
    steps = jnp.asarray(np.concatenate([steps, steps], axis=0), BF16)

    dims = (blocks, slots, own, half, taps, used, depth, lags, chunk, 3)
    rows = half * used
    piece = lags // LANES // 4
    smem = pl.BlockSpec(memory_space=pltpu.SMEM)
    vmem = pl.BlockSpec(memory_space=pltpu.VMEM)
    dma = pltpu.SemaphoreType.DMA
    out = pl.pallas_call(
        functools.partial(kernel, dims),
        out_shape=jax.ShapeDtypeStruct((own, piece, LANES), F32),
        in_specs=[smem, smem, vmem, vmem, vmem, vmem],
        out_specs=vmem,
        scratch_shapes=[
            pltpu.VMEM((blocks * rows, LANES), F32),
            pltpu.VMEM((blocks, rows, LANES), BF16),
            pltpu.VMEM((blocks, rows, LANES), BF16),
            pltpu.VMEM((pairs, half, SHIFTS, depth), BF16),
            pltpu.VMEM((pairs, half, LANES), F32),
            pltpu.VMEM((rows + 8, LANES), F32),
            pltpu.VMEM((TURNS - 1, rows + 8, LANES), F32),
            pltpu.VMEM((rows, LANES), F32),
            pltpu.VMEM((rows, LANES), F32),
            pltpu.VMEM((rows, LANES), F32),
            pltpu.VMEM((half, TURNS * TURNS, SHIFTS, LANES), BF16),
            pltpu.VMEM((half, SHIFTS, lags // SHIFTS), F32),
            pltpu.VMEM((blocks * slots, SHIFTS, lags // SHIFTS), F32),
            pltpu.VMEM((own, lags // LANES, LANES), F32),
            pltpu.VMEM((2, own, piece, LANES), F32),
            pltpu.VMEM((own, piece, LANES), F32),
            pltpu.VMEM((own, piece, LANES), F32),
            pltpu.VMEM((8, LANES), F32),
            dma((blocks,)),
            dma((blocks,)),
            dma((own // chunk, 2)),
            dma((own // chunk, 2)),
            dma((own // chunk,)),
            dma((own // chunk,)),
        ],
        compiler_params=pltpu.CompilerParams(
            collective_id=0, has_side_effects=True, vmem_limit_bytes=56 * 1024 * 1024
        ),
        name="detect",
    )(order, place, select, wave, templates, steps)
    return out.reshape(own, -1)


def solution(mesh):
    in_specs = (
        P("st", None, None),
        P("st", "ch", None),
        P("ch", None, None),
        P("ch", None, None, None),
    )
    return jax.shard_map(
        per_device, mesh=mesh, in_specs=in_specs, out_specs=P("st", "ch"), check_vma=False
    )
```

```python
import functools

import jax
import jax.numpy as jnp
import numpy as np
from jax import lax
from jax.experimental import pallas as pl
from jax.experimental.pallas import tpu as pltpu
from jax.sharding import PartitionSpec as P

EPSILON = 1e-05
SHIFTS = 16
LANES = 128
TURNS = LANES // SHIFTS
STEP = 4
HALVES = 64
MOST = 32767.0
TINY = 1e-30
MESH = pl.DeviceIdType.MESH
F32 = jnp.float32
BF16 = jnp.bfloat16


def flipped(me, i, size):
    out, k = 0, 1
    while k < size:
        out = out + k * lax.rem(lax.div(me, k) + lax.div(i, k), 2)
        k *= 2
    return out


def kernel(
    dims,
    traces_ref,
    named_ref,
    wave_ref,
    filters_ref,
    steps_ref,
    out_ref,
    chosen,
    tables,
    table,
    stage,
    send,
    recv,
    skew,
    gains,
    plain,
    rolled,
    suffix,
    before,
    total,
    right,
    scale,
    parts,
    turned,
    near_recv,
    far_send,
    far_recv,
    peaks_send,
    peaks_recv,
    summed,
    table_sem,
    peaks_send_sem,
    peaks_recv_sem,
    send_sem,
    recv_sem,
    near_send_sem,
    near_recv_sem,
    far_send_sem,
    far_recv_sem,
):
    blocks, slots, templates, half, taps, used, depth, lags, chunk, lag = dims
    me = lax.axis_index("st")
    mine = lax.axis_index("ch")
    near, far = flipped(mine, 1, 4), flipped(mine, 2, 4)
    rows = half * used

    barrier = pltpu.get_barrier_semaphore()

    def greet(i, carry):
        pl.semaphore_signal(
            barrier, inc=1, device_id={"st": flipped(me, i, blocks)}, device_id_type=MESH
        )
        return carry

    lax.fori_loop(1, blocks, greet, 0)
    for other in (near, far):
        pl.semaphore_signal(barrier, inc=1, device_id={"ch": other}, device_id_type=MESH)

    comps, stations, _ = wave_ref.shape
    listed = lax.broadcasted_iota(jnp.int32, (half, stations * comps), 1)
    listed = lax.rem(listed, stations) * comps + lax.div(listed, stations)
    column = lax.broadcasted_iota(jnp.int32, (half, blocks), 1)

    def choose(owner, carry):
        wanted = jnp.where(column == me, traces_ref[owner], 0).astype(F32)
        wanted = jnp.sum(wanted, axis=1, keepdims=True)
        chosen[pl.ds(owner * half, half), :] = (wanted == listed.astype(F32)).astype(F32)
        return carry

    lax.fori_loop(0, blocks, choose, 0)
    select = chosen[...].astype(BF16)
    wide = 4 * LANES

    def gather(i, carry):
        at = pl.ds(pl.multiple_of(i * wide, wide), wide)
        wave = wave_ref[:, :, at].reshape(comps * stations, wide)
        tile = jnp.dot(select, wave, preferred_element_type=F32)
        for j in range(4):
            spots = pl.ds(i * 4 + j, blocks * half, stride=used)
            stage[spots, :] = tile[:, j * LANES : (j + 1) * LANES]
        return carry

    lax.fori_loop(0, used * LANES // wide, gather, 0)

    def staged(block):
        return stage[pl.ds(pl.multiple_of(block * rows, 16), rows), :].astype(BF16)

    pl.semaphore_wait(barrier, blocks + 1)

    def trace_copy(i):
        other = flipped(me, i, blocks)
        return pltpu.make_async_remote_copy(
            src_ref=send.at[other],
            dst_ref=recv.at[me],
            send_sem=send_sem.at[i],
            recv_sem=recv_sem.at[i],
            device_id={"st": other},
            device_id_type=MESH,
        )

    def post(i, carry):
        other = flipped(me, i, blocks)
        send[other] = staged(other)
        trace_copy(i).start()
        return carry

    lax.fori_loop(1, blocks, post, 0)

    names = named_ref[...].astype(F32)
    every = names.shape[1]
    names = jnp.concatenate([names, jnp.zeros((6, every), F32)], axis=0).astype(BF16)
    pair = lax.broadcasted_iota(jnp.int32, (LANES, every), 0)
    spot = lax.broadcasted_iota(jnp.int32, (LANES, every), 1)
    by_column, by_row = [], []
    for h in range(2):
        own = (pair >= h * HALVES) & (pair < h * HALVES + templates)
        own = own & (spot == me * templates + pair - h * HALVES)
        own = own.astype(F32).astype(BF16)
        contract = (((1,), (1,)), ((), ()))
        by_column.append(
            lax.dot_general(own, names, contract, preferred_element_type=F32)[:, h : h + 1]
        )
        by_row.append(
            lax.dot_general(names, own, contract, preferred_element_type=F32)[h : h + 1]
        )
    by_column, by_row = by_column[0] + by_column[1], by_row[0] + by_row[1]
    down = lax.broadcasted_iota(jnp.int32, (LANES, LANES), 0)
    along = lax.broadcasted_iota(jnp.int32, (LANES, LANES), 1)
    same = by_column == by_row
    good_down = lax.rem(down, HALVES) < templates
    good_along = lax.rem(along, HALVES) < templates
    ranked = jnp.sum((same & (along < down) & good_along).astype(F32), axis=1, keepdims=True)
    place = by_column * slots + ranked
    slot = lax.broadcasted_iota(jnp.int32, (LANES, 2 * LANES), 1).astype(F32)
    valid = lax.rem(lax.broadcasted_iota(jnp.int32, (LANES, 2 * LANES), 0), HALVES) < templates
    holds = ((slot == place) & valid).astype(F32).astype(BF16)
    ids = lax.broadcasted_iota(jnp.int32, (8, LANES), 1).astype(F32).astype(BF16)
    order = jnp.dot(ids, holds, preferred_element_type=F32)
    tables[:, : 2 * LANES] = order.astype(jnp.int32)
    ranked = jnp.sum((same & (down < along) & good_down).astype(F32), axis=0, keepdims=True)
    place = by_row * slots + ranked
    tables[:, 2 * LANES :] = jnp.broadcast_to(place, (8, LANES)).astype(jnp.int32)
    table_copy = pltpu.make_async_copy(tables, table, table_sem)
    table_copy.start()

    recv[me] = staged(me)

    def spread(k, carry):
        taken = filters_ref[k].astype(F32)
        mean = jnp.sum(taken * taken, axis=1, keepdims=True) / taps
        gain = 1.0 / (taps * jnp.sqrt(mean + EPSILON))
        gain = jnp.broadcast_to(gain, (2 * half, LANES))
        longer = jnp.concatenate([taken, jnp.zeros((2 * half, depth - taps), F32)], axis=1)
        for c in range(2 * half):
            wave = jnp.broadcast_to(longer[c : c + 1], (SHIFTS, depth))
            wave = pltpu.roll(wave, 0, 1, stride=1, stride_axis=0)
            skew[c // half * HALVES + k, c % half] = wave.astype(BF16)
        gains[k] = gain[:half]
        gains[HALVES + k] = gain[half:]
        return carry

    lax.fori_loop(0, templates, spread, 0)
    table_copy.wait()

    lane = lax.broadcasted_iota(jnp.int32, (SHIFTS, LANES), 1)
    low = lane < LANES // 2
    plain[rows:, :] = jnp.zeros((8, LANES), F32)
    rolled[:, rows:, :] = jnp.zeros((TURNS - 1, 8, LANES), F32)
    extra = depth // LANES

    def prepare(source):
        x = recv[source].astype(F32)
        plain[:rows, :] = x
        squares = x * x
        high = squares.astype(BF16)
        rest = (squares - high.astype(F32)).astype(BF16)
        sums = jnp.dot(
            jnp.concatenate([high, rest], axis=1), steps_ref[...], preferred_element_type=F32
        )
        suffix[:rows, :] = sums[:, :LANES]
        before[:rows, :] = sums[:, LANES : 2 * LANES]
        total[:rows, :] = sums[:, 2 * LANES :]
        for m in range(1, TURNS):
            rolled[m - 1, :rows, :] = pltpu.roll(x, LANES - SHIFTS * m, 1)
        for c in range(half):
            for m in range(TURNS):
                held = plain if m == 0 else rolled.at[m - 1]
                found = [
                    held[pl.ds(c * used + b, SHIFTS, stride=STEP), :]
                    for b in range(STEP + extra - (m == 0))
                ]
                for b in range(STEP + extra - 1):
                    tile = found[b]
                    if m > 0:
                        tile = jnp.where(lane < LANES - SHIFTS * m, tile, found[b + 1])
                    right[c, m * TURNS + b] = tile.astype(BF16)
        for c in range(0, half, 2):
            roots = []
            for d in (c, c + 1):
                for b in range(STEP):
                    base = d * used + b
                    energy = suffix[pl.ds(base, SHIFTS, stride=STEP), :]
                    for q in range(1, taps // LANES):
                        energy = energy + total[pl.ds(base + q, SHIFTS, stride=STEP), :]
                    energy = energy + before[pl.ds(base + taps // LANES, SHIFTS, stride=STEP), :]
                    roots.append(lax.rsqrt(energy / taps + EPSILON))
            roots = jnp.concatenate(roots, axis=0).T
            for t in range(TURNS // 2):
                even = roots[2 * t * SHIFTS : (2 * t + 1) * SHIFTS]
                odd = roots[(2 * t + 1) * SHIFTS : (2 * t + 2) * SHIFTS]
                at = slice(t * LANES, (t + 1) * LANES)
                scale[c, :, at] = jnp.where(low, even, pltpu.roll(odd, LANES // 2, 1))
                scale[c + 1, :, at] = jnp.where(low, pltpu.roll(even, LANES // 2, 1), odd)

    def entry(at, most):
        return jnp.minimum(jnp.maximum(table[0, at], 0), most)

    def products(source):
        base = source * slots
        chosen_pairs = [entry(base + g, 2 * HALVES - 1) for g in range(slots)]
        for c in range(half):
            left = jnp.concatenate([skew[p, c] for p in chosen_pairs], axis=0)
            tiles = []
            for m in range(TURNS):
                for b in range(STEP):
                    tiles.append(
                        jnp.concatenate(
                            [right[c, m * TURNS + b + q] for q in range(extra)], axis=1
                        )
                    )
            raw = lax.dot_general(
                left,
                jnp.concatenate(tiles, axis=0),
                (((1,), (1,)), ((), ())),
                preferred_element_type=F32,
            )
            for g in range(slots):
                gain = gains[chosen_pairs[g], pl.ds(c, 1), :]
                gain = jnp.concatenate([gain] * (lags // SHIFTS // LANES), axis=1)
                term = raw[g * SHIFTS : (g + 1) * SHIFTS] * (scale[c] * gain)
                if c == 0:
                    parts[base + g] = term
                else:
                    parts[base + g] += term

    def work(i, carry):
        source = flipped(me, i, blocks)

        @pl.when(i > 0)
        def _():
            trace_copy(i).wait_recv()

        prepare(source)
        products(source)
        return carry

    lax.fori_loop(0, blocks, work, 0)

    piece = lags // LANES // 4
    chunks = templates // chunk

    def some(j):
        return pl.ds(j * chunk, chunk)

    def spots(number):
        return pl.ds(pl.multiple_of(number * piece, 8), piece)

    def near_copy(j, side):
        number = lax.rem(near, 2) + 2 * side
        return pltpu.make_async_remote_copy(
            src_ref=turned.at[some(j), spots(number)],
            dst_ref=near_recv.at[side, some(j)],
            send_sem=near_send_sem.at[j, side],
            recv_sem=near_recv_sem.at[j, side],
            device_id={"ch": near},
            device_id_type=MESH,
        )

    def far_copy(j):
        return pltpu.make_async_remote_copy(
            src_ref=far_send.at[some(j)],
            dst_ref=far_recv.at[some(j)],
            send_sem=far_send_sem.at[j],
            recv_sem=far_recv_sem.at[j],
            device_id={"ch": far},
            device_id_type=MESH,
        )

    own_side, far_side = lax.div(mine, 2), lax.div(far, 2)

    def turn(j):
        for pair in range(chunk // 2):
            first = j * chunk + 2 * pair
            both = [
                parts[entry(2 * LANES + k, blocks * slots - 1)]
                + parts[entry(2 * LANES + HALVES + k, blocks * slots - 1)]
                for k in (first, first + 1)
            ]
            stack = []
            for t in range(TURNS // 2):
                a, b = (x[:, t * LANES : (t + 1) * LANES] for x in both)
                stack.append(jnp.where(low, a, pltpu.roll(b, LANES // 2, 1)))
                stack.append(jnp.where(low, pltpu.roll(a, LANES // 2, 1), b))
            flat = jnp.concatenate(stack, axis=0).T
            for i in range(2):
                for b in range(STEP):
                    at = (i * STEP + b) * SHIFTS
                    turned[first + i, pl.ds(b, SHIFTS, stride=STEP), :] = flat[at : at + SHIFTS]

    def peaks_copy():
        return pltpu.make_async_remote_copy(
            src_ref=peaks_send,
            dst_ref=peaks_recv,
            send_sem=peaks_send_sem,
            recv_sem=peaks_recv_sem,
            device_id={"ch": far},
            device_id_type=MESH,
        )

    def pass_on(j):
        near_copy(j, far_side).wait_recv()
        peaks = peaks_send[...]
        for i in range(chunk):
            k = j * chunk + i
            value = turned[k, spots(far)] + near_recv[far_side, k]
            peak = jnp.maximum(jnp.max(jnp.abs(value), axis=1, keepdims=True), TINY)
            far_send[k] = jnp.round(value * (MOST / peak)).astype(jnp.int32).astype(jnp.int16)
            peaks = jnp.where(lane == k, peak, peaks)
        peaks_send[...] = peaks
        far_copy(j).start()

    def reduce(j, carry):
        turn(j)
        near_copy(j, far_side).start()
        near_copy(j, own_side).start()

        @pl.when(j >= lag)
        def _():
            pass_on(j - lag)

        return carry

    peaks_send[...] = jnp.zeros((piece, LANES), F32)
    lax.fori_loop(0, chunks, reduce, 0)

    def drain(j, carry):
        pass_on(j)
        return carry

    lax.fori_loop(chunks - lag, chunks, drain, 0)
    peaks_copy().start()

    peaks_copy().wait_recv()

    def finish(j, carry):
        near_copy(j, own_side).wait_recv()
        far_copy(j).wait_recv()
        peaks = peaks_recv[...] * (1.0 / MOST)
        for i in range(chunk):
            k = j * chunk + i
            unit = jnp.sum(jnp.where(lane == k, peaks, 0.0), axis=1, keepdims=True)
            value = far_recv[k].astype(jnp.int32).astype(F32) * unit
            value = value + (turned[k, spots(mine)] + near_recv[own_side, k])
            summed[pl.ds(pl.multiple_of(k * piece, 8), piece), :] = value
        near_copy(j, far_side).wait_send()
        near_copy(j, own_side).wait_send()
        far_copy(j).wait_send()
        return carry

    lax.fori_loop(0, chunks, finish, 0)
    peaks_copy().wait_send()

    def lay(first, count):
        for r in range(piece):
            found = summed[pl.ds(first * piece + r, count, stride=piece), :]
            out_ref[pl.ds(first, count), r * LANES : (r + 1) * LANES] = found

    def lay_eight(i, carry):
        lay(pl.multiple_of(i * 8, 8), 8)
        return carry

    lax.fori_loop(0, templates // 8, lay_eight, 0)
    if templates % 8:
        lay(templates // 8 * 8, templates % 8)

    def close(i, carry):
        trace_copy(i).wait_send()
        return carry

    lax.fori_loop(1, blocks, close, 0)


def per_device(waveform, templates, block_of, trace_of):
    me = lax.axis_index("st")
    blocks = lax.axis_size("st")
    own, chans, taps = templates.shape
    half = chans // 2
    stations, comps, window = waveform.shape
    lags = window - taps
    used = window // LANES
    depth = taps + LANES
    pairs = 2 * own
    slots = -(-13 * pairs // (10 * blocks))
    chunk = 4
    assert own % chunk == 0 and lags == 64 * LANES and used % 4 == 0

    wave = jnp.transpose(waveform, (1, 0, 2))
    traces = jnp.transpose(trace_of[0], (0, 2, 1))
    named = jnp.transpose(block_of[0], (1, 0))

    spots = np.arange(LANES)
    later = spots[:, None] >= spots[None, :]
    steps = np.concatenate([later, ~later, np.ones_like(later)], axis=1)
    steps = jnp.asarray(np.concatenate([steps, steps], axis=0), BF16)

    dims = (blocks, slots, own, half, taps, used, depth, lags, chunk, 3)
    rows = half * used
    piece = lags // LANES // 4
    smem = pl.BlockSpec(memory_space=pltpu.SMEM)
    vmem = pl.BlockSpec(memory_space=pltpu.VMEM)
    dma = pltpu.SemaphoreType.DMA
    out = pl.pallas_call(
        functools.partial(kernel, dims),
        out_shape=jax.ShapeDtypeStruct((own, piece * LANES), F32),
        in_specs=[vmem] * 5,
        out_specs=vmem,
        scratch_shapes=[
            pltpu.VMEM((blocks * half, stations * comps), F32),
            pltpu.VMEM((8, 3 * LANES), jnp.int32),
            pltpu.SMEM((8, 3 * LANES), jnp.int32),
            pltpu.VMEM((blocks * rows, LANES), F32),
            pltpu.VMEM((blocks, rows, LANES), BF16),
            pltpu.VMEM((blocks, rows, LANES), BF16),
            pltpu.VMEM((2 * HALVES, half, SHIFTS, depth), BF16),
            pltpu.VMEM((2 * HALVES, half, LANES), F32),
            pltpu.VMEM((rows + 8, LANES), F32),
            pltpu.VMEM((TURNS - 1, rows + 8, LANES), F32),
            pltpu.VMEM((rows, LANES), F32),
            pltpu.VMEM((rows, LANES), F32),
            pltpu.VMEM((rows, LANES), F32),
            pltpu.VMEM((half, TURNS * TURNS, SHIFTS, LANES), BF16),
            pltpu.VMEM((half, SHIFTS, lags // SHIFTS), F32),
            pltpu.VMEM((blocks * slots, SHIFTS, lags // SHIFTS), F32),
            pltpu.VMEM((own, lags // LANES, LANES), F32),
            pltpu.VMEM((2, own, piece, LANES), F32),
            pltpu.VMEM((own, piece, LANES), jnp.int16),
            pltpu.VMEM((own, piece, LANES), jnp.int16),
            pltpu.VMEM((piece, LANES), F32),
            pltpu.VMEM((piece, LANES), F32),
            pltpu.VMEM((own * piece, LANES), F32),
            dma,
            dma,
            dma,
            dma((blocks,)),
            dma((blocks,)),
            dma((own // chunk, 2)),
            dma((own // chunk, 2)),
            dma((own // chunk,)),
            dma((own // chunk,)),
        ],
        compiler_params=pltpu.CompilerParams(
            collective_id=0, has_side_effects=True, vmem_limit_bytes=56 * 1024 * 1024
        ),
        name="detect",
    )(traces, named, wave, templates, steps)
    return out


def solution(mesh):
    in_specs = (
        P("st", None, None),
        P("st", "ch", None),
        P("ch", None, None),
        P("ch", None, None, None),
    )
    return jax.shard_map(
        per_device, mesh=mesh, in_specs=in_specs, out_specs=P("st", "ch"), check_vma=False
    )
```

```python
import functools

import jax
import jax.numpy as jnp
import numpy as np
from jax import lax
from jax.experimental import pallas as pl
from jax.experimental.pallas import tpu as pltpu
from jax.sharding import PartitionSpec as P

EPSILON = 1e-05
SHIFTS = 16
LANES = 128
TURNS = LANES // SHIFTS
STEP = 4
HALVES = 64
MOST = 32767.0
TINY = 1e-30
MESH = pl.DeviceIdType.MESH
F32 = jnp.float32
BF16 = jnp.bfloat16


def flipped(me, i, size):
    out, k = 0, 1
    while k < size:
        out = out + k * lax.rem(lax.div(me, k) + lax.div(i, k), 2)
        k *= 2
    return out


def kernel(
    dims,
    traces_hbm,
    named_hbm,
    wave_hbm,
    filters_hbm,
    steps_hbm,
    near_ref,
    far_ref,
    traces_ref,
    named_ref,
    wave_ref,
    filters_ref,
    steps_ref,
    chosen,
    tables,
    table,
    stage,
    send,
    recv,
    skew,
    gains,
    plain,
    rolled,
    suffix,
    before,
    total,
    right,
    scale,
    parts,
    turned,
    near_recv,
    far_send,
    far_recv,
    peaks_send,
    peaks_recv,
    summed,
    load_sem,
    table_sem,
    peaks_send_sem,
    peaks_recv_sem,
    send_sem,
    recv_sem,
    near_send_sem,
    near_recv_sem,
    far_send_sem,
    far_recv_sem,
):
    blocks, slots, templates, half, taps, used, depth, lags, bounds = dims
    me = lax.axis_index("st")
    mine = lax.axis_index("ch")
    near, far = flipped(mine, 1, 4), flipped(mine, 2, 4)
    rows = half * used
    window = used * LANES
    parcels = [(a * window // 4, window // 4) for a in range(4)]
    waves = [
        pltpu.make_async_copy(
            wave_hbm.at[:, :, pl.ds(*at)], wave_ref.at[:, :, pl.ds(*at)], load_sem.at[4 + a]
        )
        for a, at in enumerate(parcels)
    ]
    others = [
        pltpu.make_async_copy(held, target, load_sem.at[a])
        for a, (held, target) in enumerate(
            (
                (traces_hbm, traces_ref),
                (named_hbm, named_ref),
                (filters_hbm, filters_ref),
                (steps_hbm, steps_ref),
            )
        )
    ]
    others[0].start()
    for copy in waves + others[1:]:
        copy.start()

    barrier = pltpu.get_barrier_semaphore()

    def greet(i, carry):
        pl.semaphore_signal(
            barrier, inc=1, device_id={"st": flipped(me, i, blocks)}, device_id_type=MESH
        )
        return carry

    lax.fori_loop(1, blocks, greet, 0)
    for other in (near, far):
        pl.semaphore_signal(barrier, inc=1, device_id={"ch": other}, device_id_type=MESH)

    comps, stations, _ = wave_ref.shape
    listed = lax.broadcasted_iota(jnp.int32, (half, stations * comps), 1)
    listed = lax.rem(listed, stations) * comps + lax.div(listed, stations)
    column = lax.broadcasted_iota(jnp.int32, (half, blocks), 1)

    def choose(owner, carry):
        wanted = jnp.where(column == me, traces_ref[owner], 0).astype(F32)
        wanted = jnp.sum(wanted, axis=1, keepdims=True)
        chosen[pl.ds(owner * half, half), :] = (wanted == listed.astype(F32)).astype(F32)
        return carry

    others[0].wait()
    lax.fori_loop(0, blocks, choose, 0)
    select = chosen[...].astype(BF16)
    wide = LANES

    def gather(i, carry):
        at = pl.ds(pl.multiple_of(i * wide, wide), wide)
        wave = wave_ref[:, :, at].reshape(comps * stations, wide)
        tile = jnp.dot(select, wave, preferred_element_type=F32)
        stage[pl.ds(i, blocks * half, stride=used), :] = tile
        return carry

    for a, copy in enumerate(waves):
        copy.wait()
        lax.fori_loop(a * used // 4, (a + 1) * used // 4, gather, 0, unroll=True)

    def staged(block):
        return stage[pl.ds(pl.multiple_of(block * rows, 16), rows), :].astype(BF16)

    pl.semaphore_wait(barrier, blocks + 1)

    def trace_copy(i):
        other = flipped(me, i, blocks)
        return pltpu.make_async_remote_copy(
            src_ref=send.at[other],
            dst_ref=recv.at[me],
            send_sem=send_sem.at[i],
            recv_sem=recv_sem.at[i],
            device_id={"st": other},
            device_id_type=MESH,
        )

    def post(i, carry):
        other = flipped(me, i, blocks)
        send[other] = staged(other)
        trace_copy(i).start()
        return carry

    first_wave = blocks * 3 // 4
    lax.fori_loop(1, first_wave, post, 0)

    for copy in others[1:]:
        copy.wait()
    names = named_ref[...].astype(F32)
    every = names.shape[1]
    names = jnp.concatenate([names, jnp.zeros((6, every), F32)], axis=0).astype(BF16)
    pair = lax.broadcasted_iota(jnp.int32, (LANES, every), 0)
    spot = lax.broadcasted_iota(jnp.int32, (LANES, every), 1)
    by_column, by_row = [], []
    for h in range(2):
        own = (pair >= h * HALVES) & (pair < h * HALVES + templates)
        own = own & (spot == me * templates + pair - h * HALVES)
        own = own.astype(F32).astype(BF16)
        contract = (((1,), (1,)), ((), ()))
        by_column.append(
            lax.dot_general(own, names, contract, preferred_element_type=F32)[:, h : h + 1]
        )
        by_row.append(
            lax.dot_general(names, own, contract, preferred_element_type=F32)[h : h + 1]
        )
    by_column, by_row = by_column[0] + by_column[1], by_row[0] + by_row[1]
    down = lax.broadcasted_iota(jnp.int32, (LANES, LANES), 0)
    along = lax.broadcasted_iota(jnp.int32, (LANES, LANES), 1)
    same = by_column == by_row
    good_down = lax.rem(down, HALVES) < templates
    good_along = lax.rem(along, HALVES) < templates
    ranked = jnp.sum((same & (along < down) & good_along).astype(F32), axis=1, keepdims=True)
    place = by_column * slots + ranked
    slot = lax.broadcasted_iota(jnp.int32, (LANES, 2 * LANES), 1).astype(F32)
    valid = lax.rem(lax.broadcasted_iota(jnp.int32, (LANES, 2 * LANES), 0), HALVES) < templates
    holds = ((slot == place) & valid).astype(F32).astype(BF16)
    ids = lax.broadcasted_iota(jnp.int32, (8, LANES), 1).astype(F32).astype(BF16)
    order = jnp.dot(ids, holds, preferred_element_type=F32)
    tables[:, : 2 * LANES] = order.astype(jnp.int32)
    ranked = jnp.sum((same & (down < along) & good_down).astype(F32), axis=0, keepdims=True)
    place = by_row * slots + ranked
    tables[:, 2 * LANES :] = jnp.broadcast_to(place, (8, LANES)).astype(jnp.int32)
    table_copy = pltpu.make_async_copy(tables, table, table_sem)
    table_copy.start()

    recv[me] = staged(me)

    def spread(k, carry):
        taken = filters_ref[k].astype(F32)
        mean = jnp.sum(taken * taken, axis=1, keepdims=True) / taps
        gain = 1.0 / (taps * jnp.sqrt(mean + EPSILON))
        gain = jnp.broadcast_to(gain, (2 * half, LANES))
        longer = jnp.concatenate([taken, jnp.zeros((2 * half, depth - taps), F32)], axis=1)
        for c in range(2 * half):
            wave = jnp.broadcast_to(longer[c : c + 1], (SHIFTS, depth))
            wave = pltpu.roll(wave, 0, 1, stride=1, stride_axis=0)
            skew[c // half * HALVES + k, c % half] = wave.astype(BF16)
        gains[k] = gain[:half]
        gains[HALVES + k] = gain[half:]
        return carry

    lax.fori_loop(0, templates, spread, 0)
    table_copy.wait()

    lane = lax.broadcasted_iota(jnp.int32, (SHIFTS, LANES), 1)
    low = lane < LANES // 2
    plain[rows:, :] = jnp.zeros((8, LANES), F32)
    rolled[:, rows:, :] = jnp.zeros((TURNS - 1, 8, LANES), F32)
    extra = depth // LANES

    def prepare(source):
        x = recv[source].astype(F32)
        plain[:rows, :] = x
        squares = x * x
        high = squares.astype(BF16)
        rest = (squares - high.astype(F32)).astype(BF16)
        sums = jnp.dot(
            jnp.concatenate([high, rest], axis=1), steps_ref[...], preferred_element_type=F32
        )
        suffix[:rows, :] = sums[:, :LANES]
        before[:rows, :] = sums[:, LANES : 2 * LANES]
        total[:rows, :] = sums[:, 2 * LANES :]
        for m in range(1, TURNS):
            rolled[m - 1, :rows, :] = pltpu.roll(x, LANES - SHIFTS * m, 1)
        for c in range(half):
            for m in range(TURNS):
                held = plain if m == 0 else rolled.at[m - 1]
                found = [
                    held[pl.ds(c * used + b, SHIFTS, stride=STEP), :]
                    for b in range(STEP + extra - (m == 0))
                ]
                for b in range(STEP + extra - 1):
                    tile = found[b]
                    if m > 0:
                        tile = jnp.where(lane < LANES - SHIFTS * m, tile, found[b + 1])
                    right[c, m * TURNS + b] = tile.astype(BF16)
        for c in range(0, half, 2):
            roots = []
            for d in (c, c + 1):
                for b in range(STEP):
                    base = d * used + b
                    energy = suffix[pl.ds(base, SHIFTS, stride=STEP), :]
                    for q in range(1, taps // LANES):
                        energy = energy + total[pl.ds(base + q, SHIFTS, stride=STEP), :]
                    energy = energy + before[pl.ds(base + taps // LANES, SHIFTS, stride=STEP), :]
                    roots.append(lax.rsqrt(energy / taps + EPSILON))
            roots = jnp.concatenate(roots, axis=0).T
            for t in range(TURNS // 2):
                even = roots[2 * t * SHIFTS : (2 * t + 1) * SHIFTS]
                odd = roots[(2 * t + 1) * SHIFTS : (2 * t + 2) * SHIFTS]
                at = slice(t * LANES, (t + 1) * LANES)
                scale[c, :, at] = jnp.where(low, even, pltpu.roll(odd, LANES // 2, 1))
                scale[c + 1, :, at] = jnp.where(low, pltpu.roll(even, LANES // 2, 1), odd)

    def entry(at, most):
        return jnp.minimum(jnp.maximum(table[0, at], 0), most)

    def products(source):
        base = source * slots
        chosen_pairs = [entry(base + g, 2 * HALVES - 1) for g in range(slots)]
        for c in range(half):
            left = jnp.concatenate([skew[p, c] for p in chosen_pairs], axis=0)
            tiles = []
            for m in range(TURNS):
                for b in range(STEP):
                    tiles.append(
                        jnp.concatenate(
                            [right[c, m * TURNS + b + q] for q in range(extra)], axis=1
                        )
                    )
            raw = lax.dot_general(
                left,
                jnp.concatenate(tiles, axis=0),
                (((1,), (1,)), ((), ())),
                preferred_element_type=F32,
            )
            for g in range(slots):
                gain = gains[chosen_pairs[g], pl.ds(c, 1), :]
                gain = jnp.concatenate([gain] * (lags // SHIFTS // LANES), axis=1)
                term = raw[g * SHIFTS : (g + 1) * SHIFTS] * (scale[c] * gain)
                if c == 0:
                    parts[base + g] = term
                else:
                    parts[base + g] += term

    def close(i, carry):
        trace_copy(i).wait_send()
        return carry

    def work(i, carry):
        source = flipped(me, i, blocks)

        @pl.when(i == 2)
        def _():
            lax.fori_loop(blocks // 2, first_wave, close, 0)
            lax.fori_loop(first_wave, blocks, post, 0)

        @pl.when(i > 0)
        def _():
            trace_copy(i).wait_recv()

        prepare(source)
        products(source)
        return carry

    lax.fori_loop(0, blocks, work, 0)

    piece = lags // LANES // 4
    own_side, far_side = lax.div(mine, 2), lax.div(far, 2)

    def some(j):
        return pl.ds(bounds[j], bounds[j + 1] - bounds[j])

    def spots(number):
        return pl.ds(pl.multiple_of(number * piece, 8), piece)

    def near_copy(j, side):
        number = lax.rem(near, 2) + 2 * side
        return pltpu.make_async_remote_copy(
            src_ref=turned.at[some(j), spots(number)],
            dst_ref=near_recv.at[side, some(j)],
            send_sem=near_send_sem.at[j, side],
            recv_sem=near_recv_sem.at[j, side],
            device_id={"ch": near},
            device_id_type=MESH,
        )

    def far_copy(j):
        return pltpu.make_async_remote_copy(
            src_ref=far_send.at[some(j)],
            dst_ref=far_recv.at[some(j)],
            send_sem=far_send_sem.at[j],
            recv_sem=far_recv_sem.at[j],
            device_id={"ch": far},
            device_id_type=MESH,
        )

    def peaks_copy(j):
        return pltpu.make_async_remote_copy(
            src_ref=peaks_send.at[j],
            dst_ref=peaks_recv.at[j],
            send_sem=peaks_send_sem.at[j],
            recv_sem=peaks_recv_sem.at[j],
            device_id={"ch": far},
            device_id_type=MESH,
        )

    def turn(j, carry):
        both = []
        for i in range(2):
            k = 2 * j + i
            both.append(
                parts[entry(2 * LANES + k, blocks * slots - 1)]
                + parts[entry(2 * LANES + HALVES + k, blocks * slots - 1)]
            )
        stack = []
        for t in range(TURNS // 2):
            a, b = (x[:, t * LANES : (t + 1) * LANES] for x in both)
            stack.append(jnp.where(low, a, pltpu.roll(b, LANES // 2, 1)))
            stack.append(jnp.where(low, pltpu.roll(a, LANES // 2, 1), b))
        flat = jnp.concatenate(stack, axis=0).T
        for i in range(2):
            for b in range(STEP):
                at = (i * STEP + b) * SHIFTS
                turned[2 * j + i, pl.ds(b, SHIFTS, stride=STEP), :] = flat[at : at + SHIFTS]
        return carry

    def pass_on(j):
        near_copy(j, far_side).wait_recv()
        value = turned[some(j), spots(far)] + near_recv[far_side, some(j)]
        tiles = value.reshape(-1, 8, LANES)
        peak = jnp.maximum(jnp.max(jnp.abs(tiles), axis=0), TINY)
        peaks_send[j] = peak
        peaks_copy(j).start()
        whole = jnp.round(tiles * (MOST / peak)[None]).astype(jnp.int32)
        far_send[some(j)] = whole.reshape(value.shape).astype(jnp.int16)
        far_copy(j).start()

    def lay(target, j, value):
        first, count = bounds[j], bounds[j + 1] - bounds[j]
        summed[: count * piece, :] = value.reshape(count * piece, LANES)
        for k in range(0, count, 8):
            size = min(8, count - k)
            for r in range(piece):
                found = summed[pl.ds(k * piece + r, size, stride=piece), :]
                target[first + k : first + k + size, r * LANES : (r + 1) * LANES] = found

    pieces = len(bounds) - 1
    for j in range(pieces):
        lax.fori_loop(bounds[j] // 2, bounds[j + 1] // 2, turn, 0, unroll=2)
        near_copy(j, far_side).start()
        near_copy(j, own_side).start()
        if j > 0:
            pass_on(j - 1)
    pass_on(pieces - 1)
    for j in range(pieces):
        near_copy(j, own_side).wait_recv()
        lay(near_ref, j, turned[some(j), spots(mine)] + near_recv[own_side, some(j)])
    for j in range(pieces):
        peaks_copy(j).wait_recv()
        far_copy(j).wait_recv()
        whole = far_recv[some(j)].astype(jnp.int32).astype(F32)
        tiles = whole.reshape(-1, 8, LANES) * (peaks_recv[j] * (1.0 / MOST))[None]
        lay(far_ref, j, tiles)
    for j in range(pieces):
        near_copy(j, far_side).wait_send()
        near_copy(j, own_side).wait_send()
        far_copy(j).wait_send()
        peaks_copy(j).wait_send()

    lax.fori_loop(1, blocks // 2, close, 0)
    lax.fori_loop(first_wave, blocks, close, 0)


def per_device(waveform, templates, block_of, trace_of):
    me = lax.axis_index("st")
    blocks = lax.axis_size("st")
    own, chans, taps = templates.shape
    half = chans // 2
    stations, comps, window = waveform.shape
    lags = window - taps
    used = window // LANES
    depth = taps + LANES
    pairs = 2 * own
    slots = -(-13 * pairs // (10 * blocks))
    bounds = (0, 8, 24, 40, own)
    count = len(bounds) - 1
    assert 40 < own <= HALVES and own % 2 == 0 and lags == 64 * LANES and used % 4 == 0

    wave = jnp.transpose(waveform, (1, 0, 2))
    traces = jnp.transpose(trace_of[0], (0, 2, 1))
    named = jnp.transpose(block_of[0], (1, 0))

    spots = np.arange(LANES)
    later = spots[:, None] >= spots[None, :]
    steps = np.concatenate([later, ~later, np.ones_like(later)], axis=1)
    steps = jnp.asarray(np.concatenate([steps, steps], axis=0), BF16)

    dims = (blocks, slots, own, half, taps, used, depth, lags, bounds)
    rows = half * used
    piece = lags // LANES // 4
    smem = pl.BlockSpec(memory_space=pltpu.SMEM)
    vmem = pl.BlockSpec(memory_space=pltpu.VMEM)
    dma = pltpu.SemaphoreType.DMA
    given = (traces, named, wave, templates, steps)
    given = [pltpu.with_memory_space_constraint(x, pltpu.HBM) for x in given]
    near, far = pl.pallas_call(
        functools.partial(kernel, dims),
        out_shape=[pltpu.VMEM((own, piece * LANES), F32)] * 2,
        in_specs=[pl.BlockSpec(memory_space=pltpu.HBM)] * 5,
        out_specs=[vmem, vmem],
        scratch_shapes=[
            pltpu.VMEM(traces.shape, jnp.int32),
            pltpu.VMEM(named.shape, jnp.int32),
            pltpu.VMEM(wave.shape, BF16),
            pltpu.VMEM(templates.shape, BF16),
            pltpu.VMEM(steps.shape, BF16),
            pltpu.VMEM((blocks * half, stations * comps), F32),
            pltpu.VMEM((8, 3 * LANES), jnp.int32),
            pltpu.SMEM((8, 3 * LANES), jnp.int32),
            pltpu.VMEM((blocks * rows, LANES), F32),
            pltpu.VMEM((blocks, rows, LANES), BF16),
            pltpu.VMEM((blocks, rows, LANES), BF16),
            pltpu.VMEM((2 * HALVES, half, SHIFTS, depth), BF16),
            pltpu.VMEM((2 * HALVES, half, LANES), F32),
            pltpu.VMEM((rows + 8, LANES), F32),
            pltpu.VMEM((TURNS - 1, rows + 8, LANES), F32),
            pltpu.VMEM((rows, LANES), F32),
            pltpu.VMEM((rows, LANES), F32),
            pltpu.VMEM((rows, LANES), F32),
            pltpu.VMEM((half, TURNS * TURNS, SHIFTS, LANES), BF16),
            pltpu.VMEM((half, SHIFTS, lags // SHIFTS), F32),
            pltpu.VMEM((blocks * slots, SHIFTS, lags // SHIFTS), F32),
            pltpu.VMEM((own, lags // LANES, LANES), F32),
            pltpu.VMEM((2, own, piece, LANES), F32),
            pltpu.VMEM((own, piece, LANES), jnp.int16),
            pltpu.VMEM((own, piece, LANES), jnp.int16),
            pltpu.VMEM((count, 8, LANES), F32),
            pltpu.VMEM((count, 8, LANES), F32),
            pltpu.VMEM((16 * piece, LANES), F32),
            dma((8,)),
            dma,
            dma((count,)),
            dma((count,)),
            dma((blocks,)),
            dma((blocks,)),
            dma((count, 2)),
            dma((count, 2)),
            dma((count,)),
            dma((count,)),
        ],
        compiler_params=pltpu.CompilerParams(
            collective_id=0, has_side_effects=True, vmem_limit_bytes=(52 + blocks) * 512 * 1024
        ),
        name="detect",
    )(*given)
    return near + far


def solution(mesh):
    in_specs = (
        P("st", None, None),
        P("st", "ch", None),
        P("ch", None, None),
        P("ch", None, None, None),
    )
    return jax.shard_map(
        per_device, mesh=mesh, in_specs=in_specs, out_specs=P("st", "ch"), check_vma=False
    )
```

```python
import functools

import jax
import jax.numpy as jnp
import numpy as np
from jax import lax
from jax.experimental import pallas as pl
from jax.experimental.pallas import tpu as pltpu
from jax.sharding import PartitionSpec as P

EPSILON = 1e-05
SHIFTS = 16
LANES = 128
TURNS = LANES // SHIFTS
STEP = 4
HALVES = 64
UNROLL = 4
MOST = 32767.0
TINY = 1e-30
MESH = pl.DeviceIdType.MESH
F32 = jnp.float32
BF16 = jnp.bfloat16


def flipped(me, i, size):
    out, k = 0, 1
    while k < size:
        out = out + k * lax.rem(lax.div(me, k) + lax.div(i, k), 2)
        k *= 2
    return out


def kernel(
    dims,
    traces_hbm,
    named_hbm,
    wave_hbm,
    filters_hbm,
    steps_hbm,
    near_ref,
    far_ref,
    traces_ref,
    named_ref,
    wave_ref,
    filters_ref,
    steps_ref,
    chosen,
    tables,
    table,
    stage,
    send,
    recv,
    skew,
    gains,
    plain,
    rolled,
    suffix,
    before,
    total,
    right,
    scale,
    parts,
    turned,
    near_recv,
    far_send,
    far_recv,
    peaks_send,
    peaks_recv,
    summed,
    load_sem,
    table_sem,
    peaks_send_sem,
    peaks_recv_sem,
    send_sem,
    recv_sem,
    near_send_sem,
    near_recv_sem,
    far_send_sem,
    far_recv_sem,
):
    blocks, slots, templates, half, taps, used, depth, lags, bounds = dims
    me = lax.axis_index("st")
    mine = lax.axis_index("ch")
    near, far = flipped(mine, 1, 4), flipped(mine, 2, 4)
    rows = half * used
    window = used * LANES
    parcels = [(a * window // 4, window // 4) for a in range(4)]
    waves = [
        pltpu.make_async_copy(
            wave_hbm.at[:, :, pl.ds(*at)], wave_ref.at[:, :, pl.ds(*at)], load_sem.at[4 + a]
        )
        for a, at in enumerate(parcels)
    ]
    others = [
        pltpu.make_async_copy(held, target, load_sem.at[a])
        for a, (held, target) in enumerate(
            (
                (traces_hbm, traces_ref),
                (named_hbm, named_ref),
                (filters_hbm, filters_ref),
                (steps_hbm, steps_ref),
            )
        )
    ]
    others[0].start()
    for copy in waves + others[1:]:
        copy.start()

    barrier = pltpu.get_barrier_semaphore()

    def greet(i, carry):
        pl.semaphore_signal(
            barrier, inc=1, device_id={"st": flipped(me, i, blocks)}, device_id_type=MESH
        )
        return carry

    lax.fori_loop(1, blocks, greet, 0)
    for other in (near, far):
        pl.semaphore_signal(barrier, inc=1, device_id={"ch": other}, device_id_type=MESH)

    comps, stations, _ = wave_ref.shape
    listed = lax.broadcasted_iota(jnp.int32, (half, stations * comps), 1)
    listed = lax.rem(listed, stations) * comps + lax.div(listed, stations)
    column = lax.broadcasted_iota(jnp.int32, (half, blocks), 1)

    def choose(owner, carry):
        wanted = jnp.where(column == me, traces_ref[owner], 0).astype(F32)
        wanted = jnp.sum(wanted, axis=1, keepdims=True)
        chosen[pl.ds(owner * half, half), :] = (wanted == listed.astype(F32)).astype(F32)
        return carry

    others[0].wait()
    lax.fori_loop(0, blocks, choose, 0)
    select = chosen[...].astype(BF16)
    wide = LANES

    def gather(i, carry):
        at = pl.ds(pl.multiple_of(i * wide, wide), wide)
        wave = wave_ref[:, :, at].reshape(comps * stations, wide)
        tile = jnp.dot(select, wave, preferred_element_type=F32)
        stage[pl.ds(i, blocks * half, stride=used), :] = tile
        return carry

    for a, copy in enumerate(waves):
        copy.wait()
        lax.fori_loop(a * used // 4, (a + 1) * used // 4, gather, 0, unroll=True)

    def staged(block):
        return stage[pl.ds(pl.multiple_of(block * rows, 16), rows), :].astype(BF16)

    pl.semaphore_wait(barrier, blocks + 1)

    def trace_copy(i):
        other = flipped(me, i, blocks)
        return pltpu.make_async_remote_copy(
            src_ref=send.at[other],
            dst_ref=recv.at[me],
            send_sem=send_sem.at[i],
            recv_sem=recv_sem.at[i],
            device_id={"st": other},
            device_id_type=MESH,
        )

    def post(i, carry):
        other = flipped(me, i, blocks)
        send[other] = staged(other)
        trace_copy(i).start()
        return carry

    first_wave = blocks * 3 // 4
    lax.fori_loop(1, first_wave, post, 0)

    for copy in others[1:]:
        copy.wait()
    names = named_ref[...].astype(F32)
    every = names.shape[1]
    names = jnp.concatenate([names, jnp.zeros((6, every), F32)], axis=0).astype(BF16)
    pair = lax.broadcasted_iota(jnp.int32, (LANES, every), 0)
    spot = lax.broadcasted_iota(jnp.int32, (LANES, every), 1)
    by_column, by_row = [], []
    for h in range(2):
        own = (pair >= h * HALVES) & (pair < h * HALVES + templates)
        own = own & (spot == me * templates + pair - h * HALVES)
        own = own.astype(F32).astype(BF16)
        contract = (((1,), (1,)), ((), ()))
        by_column.append(
            lax.dot_general(own, names, contract, preferred_element_type=F32)[:, h : h + 1]
        )
        by_row.append(
            lax.dot_general(names, own, contract, preferred_element_type=F32)[h : h + 1]
        )
    by_column, by_row = by_column[0] + by_column[1], by_row[0] + by_row[1]
    down = lax.broadcasted_iota(jnp.int32, (LANES, LANES), 0)
    along = lax.broadcasted_iota(jnp.int32, (LANES, LANES), 1)
    same = by_column == by_row
    good_down = lax.rem(down, HALVES) < templates
    good_along = lax.rem(along, HALVES) < templates
    ranked = jnp.sum((same & (along < down) & good_along).astype(F32), axis=1, keepdims=True)
    place = by_column * slots + ranked
    slot = lax.broadcasted_iota(jnp.int32, (LANES, 2 * LANES), 1).astype(F32)
    valid = lax.rem(lax.broadcasted_iota(jnp.int32, (LANES, 2 * LANES), 0), HALVES) < templates
    holds = ((slot == place) & valid).astype(F32).astype(BF16)
    ids = lax.broadcasted_iota(jnp.int32, (8, LANES), 1).astype(F32).astype(BF16)
    order = jnp.dot(ids, holds, preferred_element_type=F32)
    tables[:, : 2 * LANES] = order.astype(jnp.int32)
    ranked = jnp.sum((same & (down < along) & good_down).astype(F32), axis=0, keepdims=True)
    place = by_row * slots + ranked
    tables[:, 2 * LANES :] = jnp.broadcast_to(place, (8, LANES)).astype(jnp.int32)
    table_copy = pltpu.make_async_copy(tables, table, table_sem)
    table_copy.start()

    recv[me] = staged(me)

    apart = lax.broadcasted_iota(jnp.int32, (SHIFTS, LANES), 1) >= lax.broadcasted_iota(
        jnp.int32, (SHIFTS, LANES), 0
    )

    def spread(k, carry):
        taken = filters_ref[k].astype(F32)
        for c in range(2 * half):
            past = jnp.zeros((SHIFTS, LANES), F32)
            for q in range(taps // LANES + 1):
                if q < taps // LANES:
                    tile = taken[c : c + 1, q * LANES : (q + 1) * LANES]
                    tile = jnp.broadcast_to(tile, (SHIFTS, LANES))
                    tile = pltpu.roll(tile, 0, 1, stride=1, stride_axis=0)
                else:
                    tile = jnp.zeros((SHIFTS, LANES), F32)
                at = slice(q * LANES, (q + 1) * LANES)
                skew[c // half * HALVES + k, c % half, :, at] = jnp.where(
                    apart, tile, past
                ).astype(BF16)
                past = tile
        return carry

    lax.fori_loop(0, templates, spread, 0, unroll=UNROLL)

    batch = templates // 4

    def weigh(j, carry):
        for i in range(batch):
            k = j * batch + i
            taken = filters_ref[k].astype(F32)
            mean = jnp.sum(taken * taken, axis=1, keepdims=True) / taps
            gain = 1.0 / (taps * jnp.sqrt(mean + EPSILON))
            gain = jnp.broadcast_to(gain, (2 * half, LANES))
            gains[k] = gain[:half]
            gains[HALVES + k] = gain[half:]
        return carry

    lax.fori_loop(0, 4, weigh, 0)
    table_copy.wait()

    lane = lax.broadcasted_iota(jnp.int32, (SHIFTS, LANES), 1)
    low = lane < LANES // 2
    plain[rows:, :] = jnp.zeros((8, LANES), F32)
    rolled[:, rows:, :] = jnp.zeros((TURNS - 1, 8, LANES), F32)
    extra = depth // LANES

    def prepare(source):
        x = recv[source].astype(F32)
        plain[:rows, :] = x
        squares = x * x
        high = squares.astype(BF16)
        rest = (squares - high.astype(F32)).astype(BF16)
        sums = jnp.dot(
            jnp.concatenate([high, rest], axis=1), steps_ref[...], preferred_element_type=F32
        )
        suffix[:rows, :] = sums[:, :LANES]
        before[:rows, :] = sums[:, LANES : 2 * LANES]
        total[:rows, :] = sums[:, 2 * LANES :]
        for m in range(1, TURNS):
            rolled[m - 1, :rows, :] = pltpu.roll(x, LANES - SHIFTS * m, 1)
        for c in range(half):
            for m in range(TURNS):
                held = plain if m == 0 else rolled.at[m - 1]
                found = [
                    held[pl.ds(c * used + b, SHIFTS, stride=STEP), :]
                    for b in range(STEP + extra - (m == 0))
                ]
                for b in range(STEP + extra - 1):
                    tile = found[b]
                    if m > 0:
                        tile = jnp.where(lane < LANES - SHIFTS * m, tile, found[b + 1])
                    right[c, m * TURNS + b] = tile.astype(BF16)
        for c in range(0, half, 2):
            roots = []
            for d in (c, c + 1):
                for b in range(STEP):
                    base = d * used + b
                    energy = suffix[pl.ds(base, SHIFTS, stride=STEP), :]
                    for q in range(1, taps // LANES):
                        energy = energy + total[pl.ds(base + q, SHIFTS, stride=STEP), :]
                    energy = energy + before[pl.ds(base + taps // LANES, SHIFTS, stride=STEP), :]
                    roots.append(lax.rsqrt(energy / taps + EPSILON))
            roots = jnp.concatenate(roots, axis=0).T
            for t in range(TURNS // 2):
                even = roots[2 * t * SHIFTS : (2 * t + 1) * SHIFTS]
                odd = roots[(2 * t + 1) * SHIFTS : (2 * t + 2) * SHIFTS]
                at = slice(t * LANES, (t + 1) * LANES)
                scale[c, :, at] = jnp.where(low, even, pltpu.roll(odd, LANES // 2, 1))
                scale[c + 1, :, at] = jnp.where(low, pltpu.roll(even, LANES // 2, 1), odd)

    def entry(at, most):
        return jnp.minimum(jnp.maximum(table[0, at], 0), most)

    def products(source):
        base = source * slots
        chosen_pairs = [entry(base + g, 2 * HALVES - 1) for g in range(slots)]
        for c in range(half):
            left = jnp.concatenate([skew[p, c] for p in chosen_pairs], axis=0)
            tiles = []
            for m in range(TURNS):
                for b in range(STEP):
                    tiles.append(
                        jnp.concatenate(
                            [right[c, m * TURNS + b + q] for q in range(extra)], axis=1
                        )
                    )
            raw = lax.dot_general(
                left,
                jnp.concatenate(tiles, axis=0),
                (((1,), (1,)), ((), ())),
                preferred_element_type=F32,
            )
            for g in range(slots):
                gain = gains[chosen_pairs[g], pl.ds(c, 1), :]
                gain = jnp.concatenate([gain] * (lags // SHIFTS // LANES), axis=1)
                term = raw[g * SHIFTS : (g + 1) * SHIFTS] * (scale[c] * gain)
                if c == 0:
                    parts[base + g] = term
                else:
                    parts[base + g] += term

    def close(i, carry):
        trace_copy(i).wait_send()
        return carry

    def work(i, carry):
        source = flipped(me, i, blocks)

        @pl.when(i == 2)
        def _():
            lax.fori_loop(blocks // 2, first_wave, close, 0)
            lax.fori_loop(first_wave, blocks, post, 0)

        @pl.when(i > 0)
        def _():
            trace_copy(i).wait_recv()

        prepare(source)
        products(source)
        return carry

    lax.fori_loop(0, blocks, work, 0)

    piece = lags // LANES // 4
    own_side, far_side = lax.div(mine, 2), lax.div(far, 2)

    def some(j):
        return pl.ds(bounds[j], bounds[j + 1] - bounds[j])

    def spots(number):
        return pl.ds(pl.multiple_of(number * piece, 8), piece)

    def near_copy(j, side):
        number = lax.rem(near, 2) + 2 * side
        return pltpu.make_async_remote_copy(
            src_ref=turned.at[some(j), spots(number)],
            dst_ref=near_recv.at[side, some(j)],
            send_sem=near_send_sem.at[j, side],
            recv_sem=near_recv_sem.at[j, side],
            device_id={"ch": near},
            device_id_type=MESH,
        )

    def far_copy(j):
        return pltpu.make_async_remote_copy(
            src_ref=far_send.at[some(j)],
            dst_ref=far_recv.at[some(j)],
            send_sem=far_send_sem.at[j],
            recv_sem=far_recv_sem.at[j],
            device_id={"ch": far},
            device_id_type=MESH,
        )

    def peaks_copy(j):
        return pltpu.make_async_remote_copy(
            src_ref=peaks_send.at[j],
            dst_ref=peaks_recv.at[j],
            send_sem=peaks_send_sem.at[j],
            recv_sem=peaks_recv_sem.at[j],
            device_id={"ch": far},
            device_id_type=MESH,
        )

    def turn(j, carry):
        both = []
        for i in range(2):
            k = 2 * j + i
            both.append(
                parts[entry(2 * LANES + k, blocks * slots - 1)]
                + parts[entry(2 * LANES + HALVES + k, blocks * slots - 1)]
            )
        stack = []
        for t in range(TURNS // 2):
            a, b = (x[:, t * LANES : (t + 1) * LANES] for x in both)
            stack.append(jnp.where(low, a, pltpu.roll(b, LANES // 2, 1)))
            stack.append(jnp.where(low, pltpu.roll(a, LANES // 2, 1), b))
        flat = jnp.concatenate(stack, axis=0).T
        for i in range(2):
            for b in range(STEP):
                at = (i * STEP + b) * SHIFTS
                turned[2 * j + i, pl.ds(b, SHIFTS, stride=STEP), :] = flat[at : at + SHIFTS]
        return carry

    def pass_on(j):
        near_copy(j, far_side).wait_recv()
        value = turned[some(j), spots(far)] + near_recv[far_side, some(j)]
        tiles = value.reshape(-1, 8, LANES)
        peak = jnp.maximum(jnp.max(jnp.abs(tiles), axis=0), TINY)
        peaks_send[j] = peak
        peaks_copy(j).start()
        whole = jnp.round(tiles * (MOST / peak)[None]).astype(jnp.int32)
        far_send[some(j)] = whole.reshape(value.shape).astype(jnp.int16)
        far_copy(j).start()

    def lay(target, j, value):
        first, count = bounds[j], bounds[j + 1] - bounds[j]
        summed[: count * piece, :] = value.reshape(count * piece, LANES)
        for k in range(0, count, 8):
            size = min(8, count - k)
            for r in range(piece):
                found = summed[pl.ds(k * piece + r, size, stride=piece), :]
                target[first + k : first + k + size, r * LANES : (r + 1) * LANES] = found

    pieces = len(bounds) - 1
    for j in range(pieces):
        lax.fori_loop(bounds[j] // 2, bounds[j + 1] // 2, turn, 0, unroll=4)
        near_copy(j, far_side).start()
        near_copy(j, own_side).start()
        if j > 0:
            pass_on(j - 1)
    pass_on(pieces - 1)
    for j in range(pieces):
        near_copy(j, own_side).wait_recv()
        lay(near_ref, j, turned[some(j), spots(mine)] + near_recv[own_side, some(j)])
    for j in range(pieces):
        peaks_copy(j).wait_recv()
        far_copy(j).wait_recv()
        whole = far_recv[some(j)].astype(jnp.int32).astype(F32)
        tiles = whole.reshape(-1, 8, LANES) * (peaks_recv[j] * (1.0 / MOST))[None]
        lay(far_ref, j, tiles)
    for j in range(pieces):
        near_copy(j, far_side).wait_send()
        near_copy(j, own_side).wait_send()
        far_copy(j).wait_send()
        peaks_copy(j).wait_send()

    lax.fori_loop(1, blocks // 2, close, 0)
    lax.fori_loop(first_wave, blocks, close, 0)


def per_device(waveform, templates, block_of, trace_of):
    me = lax.axis_index("st")
    blocks = lax.axis_size("st")
    own, chans, taps = templates.shape
    half = chans // 2
    stations, comps, window = waveform.shape
    lags = window - taps
    used = window // LANES
    depth = taps + LANES
    pairs = 2 * own
    slots = -(-13 * pairs // (10 * blocks))
    bounds = (0, 8, 24, 40, own)
    count = len(bounds) - 1
    assert 40 < own <= HALVES and own % 4 == 0 and lags == 64 * LANES and used % 4 == 0

    wave = jnp.transpose(waveform, (1, 0, 2))
    traces = jnp.transpose(trace_of[0], (0, 2, 1))
    named = jnp.transpose(block_of[0], (1, 0))

    spots = np.arange(LANES)
    later = spots[:, None] >= spots[None, :]
    steps = np.concatenate([later, ~later, np.ones_like(later)], axis=1)
    steps = jnp.asarray(np.concatenate([steps, steps], axis=0), BF16)

    dims = (blocks, slots, own, half, taps, used, depth, lags, bounds)
    rows = half * used
    piece = lags // LANES // 4
    smem = pl.BlockSpec(memory_space=pltpu.SMEM)
    vmem = pl.BlockSpec(memory_space=pltpu.VMEM)
    dma = pltpu.SemaphoreType.DMA
    given = (traces, named, wave, templates, steps)
    given = [pltpu.with_memory_space_constraint(x, pltpu.HBM) for x in given]
    near, far = pl.pallas_call(
        functools.partial(kernel, dims),
        out_shape=[pltpu.VMEM((own, piece * LANES), F32)] * 2,
        in_specs=[pl.BlockSpec(memory_space=pltpu.HBM)] * 5,
        out_specs=[vmem, vmem],
        scratch_shapes=[
            pltpu.VMEM(traces.shape, jnp.int32),
            pltpu.VMEM(named.shape, jnp.int32),
            pltpu.VMEM(wave.shape, BF16),
            pltpu.VMEM(templates.shape, BF16),
            pltpu.VMEM(steps.shape, BF16),
            pltpu.VMEM((blocks * half, stations * comps), F32),
            pltpu.VMEM((8, 3 * LANES), jnp.int32),
            pltpu.SMEM((8, 3 * LANES), jnp.int32),
            pltpu.VMEM((blocks * rows, LANES), F32),
            pltpu.VMEM((blocks, rows, LANES), BF16),
            pltpu.VMEM((blocks, rows, LANES), BF16),
            pltpu.VMEM((2 * HALVES, half, SHIFTS, depth), BF16),
            pltpu.VMEM((2 * HALVES, half, LANES), F32),
            pltpu.VMEM((rows + 8, LANES), F32),
            pltpu.VMEM((TURNS - 1, rows + 8, LANES), F32),
            pltpu.VMEM((rows, LANES), F32),
            pltpu.VMEM((rows, LANES), F32),
            pltpu.VMEM((rows, LANES), F32),
            pltpu.VMEM((half, TURNS * TURNS, SHIFTS, LANES), BF16),
            pltpu.VMEM((half, SHIFTS, lags // SHIFTS), F32),
            pltpu.VMEM((blocks * slots, SHIFTS, lags // SHIFTS), F32),
            pltpu.VMEM((own, lags // LANES, LANES), F32),
            pltpu.VMEM((2, own, piece, LANES), F32),
            pltpu.VMEM((own, piece, LANES), jnp.int16),
            pltpu.VMEM((own, piece, LANES), jnp.int16),
            pltpu.VMEM((count, 8, LANES), F32),
            pltpu.VMEM((count, 8, LANES), F32),
            pltpu.VMEM((16 * piece, LANES), F32),
            dma((8,)),
            dma,
            dma((count,)),
            dma((count,)),
            dma((blocks,)),
            dma((blocks,)),
            dma((count, 2)),
            dma((count, 2)),
            dma((count,)),
            dma((count,)),
        ],
        compiler_params=pltpu.CompilerParams(
            collective_id=0, has_side_effects=True, vmem_limit_bytes=(52 + blocks) * 512 * 1024
        ),
        name="detect",
    )(*given)
    return near + far


def solution(mesh):
    in_specs = (
        P("st", None, None),
        P("st", "ch", None),
        P("ch", None, None),
        P("ch", None, None, None),
    )
    return jax.shard_map(
        per_device, mesh=mesh, in_specs=in_specs, out_specs=P("st", "ch"), check_vma=False
    )
```

```python
import functools

import jax
import jax.numpy as jnp
import numpy as np
from jax import lax
from jax.experimental import pallas as pl
from jax.experimental.pallas import tpu as pltpu
from jax.sharding import PartitionSpec as P

EPSILON = 1e-05
SHIFTS = 16
LANES = 128
TURNS = LANES // SHIFTS
STEP = 4
HALVES = 64
UNROLL = 13
MOST = 32767.0
TINY = 1e-30
MESH = pl.DeviceIdType.MESH
F32 = jnp.float32
BF16 = jnp.bfloat16


def flipped(me, i, size):
    out, k = 0, 1
    while k < size:
        out = out + k * lax.rem(lax.div(me, k) + lax.div(i, k), 2)
        k *= 2
    return out


def kernel(
    dims,
    traces_hbm,
    named_hbm,
    wave_hbm,
    filters_hbm,
    steps_hbm,
    near_ref,
    far_ref,
    traces_ref,
    named_ref,
    wave_ref,
    filters_ref,
    steps_ref,
    chosen,
    tables,
    table,
    stage,
    send,
    recv,
    skew,
    gains,
    plain,
    rolled,
    suffix,
    before,
    total,
    right,
    scale,
    parts,
    turned,
    near_recv,
    far_send,
    far_recv,
    peaks_send,
    peaks_recv,
    summed,
    load_sem,
    table_sem,
    peaks_send_sem,
    peaks_recv_sem,
    send_sem,
    recv_sem,
    near_send_sem,
    near_recv_sem,
    far_send_sem,
    far_recv_sem,
):
    blocks, slots, templates, half, taps, used, depth, lags, bounds = dims
    me = lax.axis_index("st")
    mine = lax.axis_index("ch")
    near, far = flipped(mine, 1, 4), flipped(mine, 2, 4)
    rows = half * used
    window = used * LANES
    parcels = [(0, window)]
    waves = [
        pltpu.make_async_copy(
            wave_hbm.at[:, :, pl.ds(*at)], wave_ref.at[:, :, pl.ds(*at)], load_sem.at[4 + a]
        )
        for a, at in enumerate(parcels)
    ]
    others = [
        pltpu.make_async_copy(held, target, load_sem.at[a])
        for a, (held, target) in enumerate(
            (
                (traces_hbm, traces_ref),
                (named_hbm, named_ref),
                (filters_hbm, filters_ref),
                (steps_hbm, steps_ref),
            )
        )
    ]
    others[0].start()
    for copy in waves + others[1:]:
        copy.start()

    barrier = pltpu.get_barrier_semaphore()

    def greet(i, carry):
        pl.semaphore_signal(
            barrier, inc=1, device_id={"st": flipped(me, i, blocks)}, device_id_type=MESH
        )
        return carry

    lax.fori_loop(1, blocks, greet, 0)
    for other in (near, far):
        pl.semaphore_signal(barrier, inc=1, device_id={"ch": other}, device_id_type=MESH)

    comps, stations, _ = wave_ref.shape
    listed = lax.broadcasted_iota(jnp.int32, (half, stations * comps), 1)
    listed = lax.rem(listed, stations) * comps + lax.div(listed, stations)
    column = lax.broadcasted_iota(jnp.int32, (half, blocks), 1)

    def choose(owner, carry):
        wanted = jnp.where(column == me, traces_ref[owner], 0).astype(F32)
        wanted = jnp.sum(wanted, axis=1, keepdims=True)
        chosen[pl.ds(owner * half, half), :] = (wanted == listed.astype(F32)).astype(F32)
        return carry

    others[0].wait()
    lax.fori_loop(0, blocks, choose, 0, unroll=8)
    select = chosen[...].astype(BF16)
    for a, copy in enumerate(waves):
        copy.wait()
        begin, size = parcels[a]
        each = size // 1
        for piece_at in range(begin, begin + size, each):
            wave = wave_ref[:, :, piece_at : piece_at + each].reshape(comps * stations, each)
            tile = jnp.dot(select, wave, preferred_element_type=F32)
            for j in range(each // LANES):
                rows_at = pl.ds(piece_at // LANES + j, blocks * half, stride=used)
                stage[rows_at, :] = tile[:, j * LANES : (j + 1) * LANES]

    def staged(block):
        return stage[pl.ds(pl.multiple_of(block * rows, 16), rows), :].astype(BF16)

    pl.semaphore_wait(barrier, blocks + 1)

    def trace_copy(i):
        other = flipped(me, i, blocks)
        return pltpu.make_async_remote_copy(
            src_ref=send.at[other],
            dst_ref=recv.at[me],
            send_sem=send_sem.at[i],
            recv_sem=recv_sem.at[i],
            device_id={"st": other},
            device_id_type=MESH,
        )

    def post(i, carry):
        other = flipped(me, i, blocks)
        send[other] = staged(other)
        trace_copy(i).start()
        return carry

    first_wave = blocks * 3 // 4
    lax.fori_loop(1, first_wave, post, 0)

    for copy in others[1:]:
        copy.wait()
    names = named_ref[...].astype(F32)
    every = names.shape[1]
    names = jnp.concatenate([names, jnp.zeros((6, every), F32)], axis=0).astype(BF16)
    pair = lax.broadcasted_iota(jnp.int32, (LANES, every), 0)
    spot = lax.broadcasted_iota(jnp.int32, (LANES, every), 1)
    by_column, by_row = [], []
    for h in range(2):
        own = (pair >= h * HALVES) & (pair < h * HALVES + templates)
        own = own & (spot == me * templates + pair - h * HALVES)
        own = own.astype(F32).astype(BF16)
        contract = (((1,), (1,)), ((), ()))
        by_column.append(
            lax.dot_general(own, names, contract, preferred_element_type=F32)[:, h : h + 1]
        )
        by_row.append(
            lax.dot_general(names, own, contract, preferred_element_type=F32)[h : h + 1]
        )
    by_column, by_row = by_column[0] + by_column[1], by_row[0] + by_row[1]
    down = lax.broadcasted_iota(jnp.int32, (LANES, LANES), 0)
    along = lax.broadcasted_iota(jnp.int32, (LANES, LANES), 1)
    same = by_column == by_row
    good_down = lax.rem(down, HALVES) < templates
    good_along = lax.rem(along, HALVES) < templates
    ranked = jnp.sum((same & (along < down) & good_along).astype(F32), axis=1, keepdims=True)
    place = by_column * slots + ranked
    slot = lax.broadcasted_iota(jnp.int32, (LANES, 2 * LANES), 1).astype(F32)
    valid = lax.rem(lax.broadcasted_iota(jnp.int32, (LANES, 2 * LANES), 0), HALVES) < templates
    holds = ((slot == place) & valid).astype(F32).astype(BF16)
    ids = lax.broadcasted_iota(jnp.int32, (8, LANES), 1).astype(F32).astype(BF16)
    order = jnp.dot(ids, holds, preferred_element_type=F32)
    tables[:, : 2 * LANES] = order.astype(jnp.int32)
    ranked = jnp.sum((same & (down < along) & good_down).astype(F32), axis=0, keepdims=True)
    place = by_row * slots + ranked
    tables[:, 2 * LANES :] = jnp.broadcast_to(place, (8, LANES)).astype(jnp.int32)
    table_copy = pltpu.make_async_copy(tables, table, table_sem)
    table_copy.start()

    recv[me] = staged(me)

    apart = lax.broadcasted_iota(jnp.int32, (SHIFTS, LANES), 1) >= lax.broadcasted_iota(
        jnp.int32, (SHIFTS, LANES), 0
    )

    def spread(k, carry):
        taken = filters_ref[k].astype(F32)
        for c in range(2 * half):
            past = jnp.zeros((SHIFTS, LANES), F32)
            for q in range(taps // LANES + 1):
                if q < taps // LANES:
                    tile = taken[c : c + 1, q * LANES : (q + 1) * LANES]
                    tile = jnp.broadcast_to(tile, (SHIFTS, LANES))
                    tile = pltpu.roll(tile, 0, 1, stride=1, stride_axis=0)
                else:
                    tile = jnp.zeros((SHIFTS, LANES), F32)
                at = slice(q * LANES, (q + 1) * LANES)
                skew[c // half * HALVES + k, c % half, :, at] = jnp.where(
                    apart, tile, past
                ).astype(BF16)
                past = tile
        return carry

    lax.fori_loop(0, templates, spread, 0, unroll=UNROLL)

    batch = templates // 4

    def weigh(j, carry):
        for i in range(batch):
            k = j * batch + i
            taken = filters_ref[k].astype(F32)
            mean = jnp.sum(taken * taken, axis=1, keepdims=True) / taps
            gain = 1.0 / (taps * jnp.sqrt(mean + EPSILON))
            gain = jnp.broadcast_to(gain, (2 * half, LANES))
            gains[k] = gain[:half]
            gains[HALVES + k] = gain[half:]
        return carry

    lax.fori_loop(0, 4, weigh, 0)
    table_copy.wait()

    lane = lax.broadcasted_iota(jnp.int32, (SHIFTS, LANES), 1)
    low = lane < LANES // 2
    plain[rows:, :] = jnp.zeros((8, LANES), F32)
    rolled[:, rows:, :] = jnp.zeros((TURNS - 1, 8, LANES), F32)
    extra = depth // LANES

    def prepare(source):
        x = recv[source].astype(F32)
        plain[:rows, :] = x
        squares = x * x
        high = squares.astype(BF16)
        rest = (squares - high.astype(F32)).astype(BF16)
        sums = jnp.dot(
            jnp.concatenate([high, rest], axis=1), steps_ref[...], preferred_element_type=F32
        )
        suffix[:rows, :] = sums[:, :LANES]
        before[:rows, :] = sums[:, LANES : 2 * LANES]
        total[:rows, :] = sums[:, 2 * LANES :]
        for m in range(1, TURNS):
            rolled[m - 1, :rows, :] = pltpu.roll(x, LANES - SHIFTS * m, 1)
        for c in range(half):
            for m in range(TURNS):
                held = plain if m == 0 else rolled.at[m - 1]
                found = [
                    held[pl.ds(c * used + b, SHIFTS, stride=STEP), :]
                    for b in range(STEP + extra - (m == 0))
                ]
                for b in range(STEP + extra - 1):
                    tile = found[b]
                    if m > 0:
                        tile = jnp.where(lane < LANES - SHIFTS * m, tile, found[b + 1])
                    right[c, m * TURNS + b] = tile.astype(BF16)
        for c in range(0, half, 2):
            roots = []
            for d in (c, c + 1):
                for b in range(STEP):
                    base = d * used + b
                    energy = suffix[pl.ds(base, SHIFTS, stride=STEP), :]
                    for q in range(1, taps // LANES):
                        energy = energy + total[pl.ds(base + q, SHIFTS, stride=STEP), :]
                    energy = energy + before[pl.ds(base + taps // LANES, SHIFTS, stride=STEP), :]
                    roots.append(lax.rsqrt(energy / taps + EPSILON))
            roots = jnp.concatenate(roots, axis=0).T
            for t in range(TURNS // 2):
                even = roots[2 * t * SHIFTS : (2 * t + 1) * SHIFTS]
                odd = roots[(2 * t + 1) * SHIFTS : (2 * t + 2) * SHIFTS]
                at = slice(t * LANES, (t + 1) * LANES)
                scale[c, :, at] = jnp.where(low, even, pltpu.roll(odd, LANES // 2, 1))
                scale[c + 1, :, at] = jnp.where(low, pltpu.roll(even, LANES // 2, 1), odd)

    def entry(at, most):
        return jnp.minimum(jnp.maximum(table[0, at], 0), most)

    def products(source):
        base = source * slots
        chosen_pairs = [entry(base + g, 2 * HALVES - 1) for g in range(slots)]
        for c in range(half):
            left = jnp.concatenate([skew[p, c] for p in chosen_pairs], axis=0)
            tiles = []
            for m in range(TURNS):
                for b in range(STEP):
                    tiles.append(
                        jnp.concatenate(
                            [right[c, m * TURNS + b + q] for q in range(extra)], axis=1
                        )
                    )
            raw = lax.dot_general(
                left,
                jnp.concatenate(tiles, axis=0),
                (((1,), (1,)), ((), ())),
                preferred_element_type=F32,
            )
            for g in range(slots):
                gain = gains[chosen_pairs[g], pl.ds(c, 1), :]
                gain = jnp.concatenate([gain] * (lags // SHIFTS // LANES), axis=1)
                term = raw[g * SHIFTS : (g + 1) * SHIFTS] * (scale[c] * gain)
                if c == 0:
                    parts[base + g] = term
                else:
                    parts[base + g] += term

    def close(i, carry):
        trace_copy(i).wait_send()
        return carry

    def work(i, carry):
        source = flipped(me, i, blocks)

        @pl.when(i == 2)
        def _():
            lax.fori_loop(blocks // 2, first_wave, close, 0)
            lax.fori_loop(first_wave, blocks, post, 0)

        @pl.when(i > 0)
        def _():
            trace_copy(i).wait_recv()

        prepare(source)
        products(source)
        return carry

    lax.fori_loop(0, blocks, work, 0)

    piece = lags // LANES // 4
    own_side, far_side = lax.div(mine, 2), lax.div(far, 2)

    def some(j):
        return pl.ds(bounds[j], bounds[j + 1] - bounds[j])

    def spots(number):
        return pl.ds(pl.multiple_of(number * piece, 8), piece)

    def near_copy(j, side):
        number = lax.rem(near, 2) + 2 * side
        return pltpu.make_async_remote_copy(
            src_ref=turned.at[some(j), spots(number)],
            dst_ref=near_recv.at[side, some(j)],
            send_sem=near_send_sem.at[j, side],
            recv_sem=near_recv_sem.at[j, side],
            device_id={"ch": near},
            device_id_type=MESH,
        )

    def far_copy(j):
        return pltpu.make_async_remote_copy(
            src_ref=far_send.at[some(j)],
            dst_ref=far_recv.at[some(j)],
            send_sem=far_send_sem.at[j],
            recv_sem=far_recv_sem.at[j],
            device_id={"ch": far},
            device_id_type=MESH,
        )

    def peaks_copy(j):
        return pltpu.make_async_remote_copy(
            src_ref=peaks_send.at[j],
            dst_ref=peaks_recv.at[j],
            send_sem=peaks_send_sem.at[j],
            recv_sem=peaks_recv_sem.at[j],
            device_id={"ch": far},
            device_id_type=MESH,
        )

    def turn(j, carry):
        both = []
        for i in range(2):
            k = 2 * j + i
            both.append(
                parts[entry(2 * LANES + k, blocks * slots - 1)]
                + parts[entry(2 * LANES + HALVES + k, blocks * slots - 1)]
            )
        stack = []
        for t in range(TURNS // 2):
            a, b = (x[:, t * LANES : (t + 1) * LANES] for x in both)
            stack.append(jnp.where(low, a, pltpu.roll(b, LANES // 2, 1)))
            stack.append(jnp.where(low, pltpu.roll(a, LANES // 2, 1), b))
        flat = jnp.concatenate(stack, axis=0).T
        for i in range(2):
            for b in range(STEP):
                at = (i * STEP + b) * SHIFTS
                turned[2 * j + i, pl.ds(b, SHIFTS, stride=STEP), :] = flat[at : at + SHIFTS]
        return carry

    def pass_on(j):
        near_copy(j, far_side).wait_recv()
        value = turned[some(j), spots(far)] + near_recv[far_side, some(j)]
        tiles = value.reshape(-1, 8, LANES)
        peak = jnp.maximum(jnp.max(jnp.abs(tiles), axis=0), TINY)
        peaks_send[j] = peak
        peaks_copy(j).start()
        whole = jnp.round(tiles * (MOST / peak)[None]).astype(jnp.int32)
        far_send[some(j)] = whole.reshape(value.shape).astype(jnp.int16)
        far_copy(j).start()

    def lay(target, j, value):
        first, count = bounds[j], bounds[j + 1] - bounds[j]
        summed[: count * piece, :] = value.reshape(count * piece, LANES)
        for k in range(0, count, 8):
            size = min(8, count - k)
            for r in range(piece):
                found = summed[pl.ds(k * piece + r, size, stride=piece), :]
                target[first + k : first + k + size, r * LANES : (r + 1) * LANES] = found

    pieces = len(bounds) - 1
    for j in range(pieces):
        lax.fori_loop(bounds[j] // 2, bounds[j + 1] // 2, turn, 0, unroll=4)
        near_copy(j, far_side).start()
        near_copy(j, own_side).start()
        if j > 0:
            pass_on(j - 1)
    pass_on(pieces - 1)
    for j in range(pieces):
        near_copy(j, own_side).wait_recv()
        lay(near_ref, j, turned[some(j), spots(mine)] + near_recv[own_side, some(j)])
    for j in range(pieces):
        peaks_copy(j).wait_recv()
        far_copy(j).wait_recv()
        whole = far_recv[some(j)].astype(jnp.int32).astype(F32)
        tiles = whole.reshape(-1, 8, LANES) * (peaks_recv[j] * (1.0 / MOST))[None]
        lay(far_ref, j, tiles)
    for j in range(pieces):
        near_copy(j, far_side).wait_send()
        near_copy(j, own_side).wait_send()
        far_copy(j).wait_send()
        peaks_copy(j).wait_send()

    lax.fori_loop(1, blocks // 2, close, 0)
    lax.fori_loop(first_wave, blocks, close, 0)


def per_device(waveform, templates, block_of, trace_of):
    me = lax.axis_index("st")
    blocks = lax.axis_size("st")
    own, chans, taps = templates.shape
    half = chans // 2
    stations, comps, window = waveform.shape
    lags = window - taps
    used = window // LANES
    depth = taps + LANES
    pairs = 2 * own
    slots = -(-13 * pairs // (10 * blocks))
    bounds = (0, 8, 24, 40, own)
    count = len(bounds) - 1
    assert 40 < own <= HALVES and own % 4 == 0 and lags == 64 * LANES and used % 4 == 0

    wave = jnp.transpose(waveform, (1, 0, 2))
    traces = jnp.transpose(trace_of[0], (0, 2, 1))
    named = jnp.transpose(block_of[0], (1, 0))

    spots = np.arange(LANES)
    later = spots[:, None] >= spots[None, :]
    steps = np.concatenate([later, ~later, np.ones_like(later)], axis=1)
    steps = jnp.asarray(np.concatenate([steps, steps], axis=0), BF16)

    dims = (blocks, slots, own, half, taps, used, depth, lags, bounds)
    rows = half * used
    piece = lags // LANES // 4
    smem = pl.BlockSpec(memory_space=pltpu.SMEM)
    vmem = pl.BlockSpec(memory_space=pltpu.VMEM)
    dma = pltpu.SemaphoreType.DMA
    given = (traces, named, wave, templates, steps)
    given = [pltpu.with_memory_space_constraint(x, pltpu.HBM) for x in given]
    near, far = pl.pallas_call(
        functools.partial(kernel, dims),
        out_shape=[pltpu.VMEM((own, piece * LANES), F32)] * 2,
        in_specs=[pl.BlockSpec(memory_space=pltpu.HBM)] * 5,
        out_specs=[vmem, vmem],
        scratch_shapes=[
            pltpu.VMEM(traces.shape, jnp.int32),
            pltpu.VMEM(named.shape, jnp.int32),
            pltpu.VMEM(wave.shape, BF16),
            pltpu.VMEM(templates.shape, BF16),
            pltpu.VMEM(steps.shape, BF16),
            pltpu.VMEM((blocks * half, stations * comps), F32),
            pltpu.VMEM((8, 3 * LANES), jnp.int32),
            pltpu.SMEM((8, 3 * LANES), jnp.int32),
            pltpu.VMEM((blocks * rows, LANES), F32),
            pltpu.VMEM((blocks, rows, LANES), BF16),
            pltpu.VMEM((blocks, rows, LANES), BF16),
            pltpu.VMEM((2 * HALVES, half, SHIFTS, depth), BF16),
            pltpu.VMEM((2 * HALVES, half, LANES), F32),
            pltpu.VMEM((rows + 8, LANES), F32),
            pltpu.VMEM((TURNS - 1, rows + 8, LANES), F32),
            pltpu.VMEM((rows, LANES), F32),
            pltpu.VMEM((rows, LANES), F32),
            pltpu.VMEM((rows, LANES), F32),
            pltpu.VMEM((half, TURNS * TURNS, SHIFTS, LANES), BF16),
            pltpu.VMEM((half, SHIFTS, lags // SHIFTS), F32),
            pltpu.VMEM((blocks * slots, SHIFTS, lags // SHIFTS), F32),
            pltpu.VMEM((own, lags // LANES, LANES), F32),
            pltpu.VMEM((2, own, piece, LANES), F32),
            pltpu.VMEM((own, piece, LANES), jnp.int16),
            pltpu.VMEM((own, piece, LANES), jnp.int16),
            pltpu.VMEM((count, 8, LANES), F32),
            pltpu.VMEM((count, 8, LANES), F32),
            pltpu.VMEM((16 * piece, LANES), F32),
            dma((8,)),
            dma,
            dma((count,)),
            dma((count,)),
            dma((blocks,)),
            dma((blocks,)),
            dma((count, 2)),
            dma((count, 2)),
            dma((count,)),
            dma((count,)),
        ],
        compiler_params=pltpu.CompilerParams(
            collective_id=0, has_side_effects=True, vmem_limit_bytes=(52 + blocks) * 512 * 1024
        ),
        name="detect",
    )(*given)
    return near + far


def solution(mesh):
    in_specs = (
        P("st", None, None),
        P("st", "ch", None),
        P("ch", None, None),
        P("ch", None, None, None),
    )
    return jax.shard_map(
        per_device, mesh=mesh, in_specs=in_specs, out_specs=P("st", "ch"), check_vma=False
    )
```

```python
import functools

import jax
import jax.numpy as jnp
import numpy as np
from jax import lax
from jax.experimental import pallas as pl
from jax.experimental.pallas import tpu as pltpu
from jax.sharding import PartitionSpec as P

EPSILON = 1e-05
SHIFTS = 16
LANES = 128
TURNS = LANES // SHIFTS
STEP = 4
HALVES = 64
UNROLL = 13
MOST = 32767.0
TINY = 1e-30
MESH = pl.DeviceIdType.MESH
F32 = jnp.float32
BF16 = jnp.bfloat16


def flipped(me, i, size):
    out, k = 0, 1
    while k < size:
        out = out + k * lax.rem(lax.div(me, k) + lax.div(i, k), 2)
        k *= 2
    return out


def kernel(
    dims,
    traces_hbm,
    named_hbm,
    wave_hbm,
    filters_hbm,
    steps_hbm,
    near_ref,
    far_ref,
    traces_ref,
    named_ref,
    wave_ref,
    filters_ref,
    steps_ref,
    chosen,
    tables,
    table,
    stage,
    send,
    recv,
    skew,
    gains,
    plain,
    rolled,
    suffix,
    before,
    total,
    right,
    scale,
    parts,
    turned,
    near_recv,
    far_send,
    far_recv,
    peaks_send,
    peaks_recv,
    summed,
    load_sem,
    table_sem,
    peaks_send_sem,
    peaks_recv_sem,
    send_sem,
    recv_sem,
    near_send_sem,
    near_recv_sem,
    far_send_sem,
    far_recv_sem,
):
    blocks, slots, templates, half, taps, used, depth, lags, bounds = dims
    me = lax.axis_index("st")
    mine = lax.axis_index("ch")
    near, far = flipped(mine, 1, 4), flipped(mine, 2, 4)
    rows = half * used
    window = used * LANES
    parcels = [(0, window)]
    waves = [
        pltpu.make_async_copy(
            wave_hbm.at[:, :, pl.ds(*at)], wave_ref.at[:, :, pl.ds(*at)], load_sem.at[4 + a]
        )
        for a, at in enumerate(parcels)
    ]
    others = [
        pltpu.make_async_copy(held, target, load_sem.at[a])
        for a, (held, target) in enumerate(
            (
                (traces_hbm, traces_ref),
                (named_hbm, named_ref),
                (filters_hbm, filters_ref),
                (steps_hbm, steps_ref),
            )
        )
    ]
    others[0].start()
    for copy in waves + others[1:]:
        copy.start()

    barrier = pltpu.get_barrier_semaphore()

    def greet(i, carry):
        pl.semaphore_signal(
            barrier, inc=1, device_id={"st": flipped(me, i, blocks)}, device_id_type=MESH
        )
        return carry

    lax.fori_loop(1, blocks, greet, 0)
    for other in (near, far):
        pl.semaphore_signal(barrier, inc=1, device_id={"ch": other}, device_id_type=MESH)

    comps, stations, _ = wave_ref.shape
    listed = lax.broadcasted_iota(jnp.int32, (half, stations * comps), 1)
    listed = lax.rem(listed, stations) * comps + lax.div(listed, stations)
    column = lax.broadcasted_iota(jnp.int32, (half, blocks), 1)

    def choose(owner, carry):
        wanted = jnp.where(column == me, traces_ref[owner], 0).astype(F32)
        wanted = jnp.sum(wanted, axis=1, keepdims=True)
        chosen[pl.ds(owner * half, half), :] = (wanted == listed.astype(F32)).astype(F32)
        return carry

    others[0].wait()
    lax.fori_loop(0, blocks, choose, 0, unroll=8)
    select = chosen[...].astype(BF16)
    for a, copy in enumerate(waves):
        copy.wait()
        begin, size = parcels[a]
        each = size // 1
        for piece_at in range(begin, begin + size, each):
            wave = wave_ref[:, :, piece_at : piece_at + each].reshape(comps * stations, each)
            tile = jnp.dot(select, wave, preferred_element_type=F32)
            for j in range(each // LANES):
                rows_at = pl.ds(piece_at // LANES + j, blocks * half, stride=used)
                stage[rows_at, :] = tile[:, j * LANES : (j + 1) * LANES]

    def staged(block):
        return stage[pl.ds(pl.multiple_of(block * rows, 16), rows), :].astype(BF16)

    pl.semaphore_wait(barrier, blocks + 1)

    def trace_copy(i):
        other = flipped(me, i, blocks)
        return pltpu.make_async_remote_copy(
            src_ref=send.at[other],
            dst_ref=recv.at[me],
            send_sem=send_sem.at[i],
            recv_sem=recv_sem.at[i],
            device_id={"st": other},
            device_id_type=MESH,
        )

    def post(i, carry):
        other = flipped(me, i, blocks)
        send[other] = staged(other)
        trace_copy(i).start()
        return carry

    first_wave = blocks * 3 // 4
    lax.fori_loop(1, first_wave, post, 0, unroll=True)

    for copy in others[1:]:
        copy.wait()
    names = named_ref[...].astype(F32)
    every = names.shape[1]
    names = jnp.concatenate([names, jnp.zeros((6, every), F32)], axis=0).astype(BF16)
    pair = lax.broadcasted_iota(jnp.int32, (LANES, every), 0)
    spot = lax.broadcasted_iota(jnp.int32, (LANES, every), 1)
    by_column, by_row = [], []
    for h in range(2):
        own = (pair >= h * HALVES) & (pair < h * HALVES + templates)
        own = own & (spot == me * templates + pair - h * HALVES)
        own = own.astype(F32).astype(BF16)
        contract = (((1,), (1,)), ((), ()))
        by_column.append(
            lax.dot_general(own, names, contract, preferred_element_type=F32)[:, h : h + 1]
        )
        by_row.append(
            lax.dot_general(names, own, contract, preferred_element_type=F32)[h : h + 1]
        )
    by_column, by_row = by_column[0] + by_column[1], by_row[0] + by_row[1]
    down = lax.broadcasted_iota(jnp.int32, (LANES, LANES), 0)
    along = lax.broadcasted_iota(jnp.int32, (LANES, LANES), 1)
    same = by_column == by_row
    good_down = lax.rem(down, HALVES) < templates
    good_along = lax.rem(along, HALVES) < templates
    ranked = jnp.sum((same & (along < down) & good_along).astype(F32), axis=1, keepdims=True)
    place = by_column * slots + ranked
    slot = lax.broadcasted_iota(jnp.int32, (LANES, 2 * LANES), 1).astype(F32)
    valid = lax.rem(lax.broadcasted_iota(jnp.int32, (LANES, 2 * LANES), 0), HALVES) < templates
    holds = ((slot == place) & valid).astype(F32).astype(BF16)
    ids = lax.broadcasted_iota(jnp.int32, (8, LANES), 1).astype(F32).astype(BF16)
    order = jnp.dot(ids, holds, preferred_element_type=F32)
    tables[:, : 2 * LANES] = order.astype(jnp.int32)
    ranked = jnp.sum((same & (down < along) & good_down).astype(F32), axis=0, keepdims=True)
    place = by_row * slots + ranked
    tables[:, 2 * LANES :] = jnp.broadcast_to(place, (8, LANES)).astype(jnp.int32)
    table_copy = pltpu.make_async_copy(tables, table, table_sem)
    table_copy.start()

    recv[me] = staged(me)

    apart = lax.broadcasted_iota(jnp.int32, (SHIFTS, LANES), 1) >= lax.broadcasted_iota(
        jnp.int32, (SHIFTS, LANES), 0
    )

    def spread(k, carry):
        taken = filters_ref[k].astype(F32)
        for c in range(2 * half):
            past = jnp.zeros((SHIFTS, LANES), F32)
            for q in range(taps // LANES + 1):
                if q < taps // LANES:
                    tile = taken[c : c + 1, q * LANES : (q + 1) * LANES]
                    tile = jnp.broadcast_to(tile, (SHIFTS, LANES))
                    tile = pltpu.roll(tile, 0, 1, stride=1, stride_axis=0)
                else:
                    tile = jnp.zeros((SHIFTS, LANES), F32)
                at = slice(q * LANES, (q + 1) * LANES)
                skew[c // half * HALVES + k, c % half, :, at] = jnp.where(
                    apart, tile, past
                ).astype(BF16)
                past = tile
        return carry

    lax.fori_loop(0, templates, spread, 0, unroll=UNROLL)

    batch = templates // 4

    def weigh(j, carry):
        for i in range(batch):
            k = j * batch + i
            taken = filters_ref[k].astype(F32)
            mean = jnp.sum(taken * taken, axis=1, keepdims=True) / taps
            gain = 1.0 / (taps * jnp.sqrt(mean + EPSILON))
            gain = jnp.broadcast_to(gain, (2 * half, LANES))
            gains[k] = gain[:half]
            gains[HALVES + k] = gain[half:]
        return carry

    lax.fori_loop(0, 4, weigh, 0)
    table_copy.wait()

    lane = lax.broadcasted_iota(jnp.int32, (SHIFTS, LANES), 1)
    low = lane < LANES // 2
    plain[rows:, :] = jnp.zeros((8, LANES), F32)
    rolled[:, rows:, :] = jnp.zeros((TURNS - 1, 8, LANES), F32)
    extra = depth // LANES

    def prepare(source):
        x = recv[source].astype(F32)
        plain[:rows, :] = x
        squares = x * x
        high = squares.astype(BF16)
        rest = (squares - high.astype(F32)).astype(BF16)
        sums = jnp.dot(
            jnp.concatenate([high, rest], axis=1), steps_ref[...], preferred_element_type=F32
        )
        suffix[:rows, :] = sums[:, :LANES]
        before[:rows, :] = sums[:, LANES : 2 * LANES]
        total[:rows, :] = sums[:, 2 * LANES :]
        for m in range(1, TURNS):
            rolled[m - 1, :rows, :] = pltpu.roll(x, LANES - SHIFTS * m, 1)
        for c in range(half):
            for m in range(TURNS):
                held = plain if m == 0 else rolled.at[m - 1]
                found = [
                    held[pl.ds(c * used + b, SHIFTS, stride=STEP), :]
                    for b in range(STEP + extra - (m == 0))
                ]
                for b in range(STEP + extra - 1):
                    tile = found[b]
                    if m > 0:
                        tile = jnp.where(lane < LANES - SHIFTS * m, tile, found[b + 1])
                    right[c, m * TURNS + b] = tile.astype(BF16)
        for c in range(0, half, 2):
            roots = []
            for d in (c, c + 1):
                for b in range(STEP):
                    base = d * used + b
                    energy = suffix[pl.ds(base, SHIFTS, stride=STEP), :]
                    for q in range(1, taps // LANES):
                        energy = energy + total[pl.ds(base + q, SHIFTS, stride=STEP), :]
                    energy = energy + before[pl.ds(base + taps // LANES, SHIFTS, stride=STEP), :]
                    roots.append(lax.rsqrt(energy / taps + EPSILON))
            roots = jnp.concatenate(roots, axis=0).T
            for t in range(TURNS // 2):
                even = roots[2 * t * SHIFTS : (2 * t + 1) * SHIFTS]
                odd = roots[(2 * t + 1) * SHIFTS : (2 * t + 2) * SHIFTS]
                at = slice(t * LANES, (t + 1) * LANES)
                scale[c, :, at] = jnp.where(low, even, pltpu.roll(odd, LANES // 2, 1))
                scale[c + 1, :, at] = jnp.where(low, pltpu.roll(even, LANES // 2, 1), odd)

    def entry(at, most):
        return jnp.minimum(jnp.maximum(table[0, at], 0), most)

    def products(source):
        base = source * slots
        chosen_pairs = [entry(base + g, 2 * HALVES - 1) for g in range(slots)]
        for c in range(half):
            left = jnp.concatenate([skew[p, c] for p in chosen_pairs], axis=0)
            tiles = []
            for m in range(TURNS):
                for b in range(STEP):
                    tiles.append(
                        jnp.concatenate(
                            [right[c, m * TURNS + b + q] for q in range(extra)], axis=1
                        )
                    )
            raw = lax.dot_general(
                left,
                jnp.concatenate(tiles, axis=0),
                (((1,), (1,)), ((), ())),
                preferred_element_type=F32,
            )
            for g in range(slots):
                gain = gains[chosen_pairs[g], pl.ds(c, 1), :]
                gain = jnp.concatenate([gain] * (lags // SHIFTS // LANES), axis=1)
                term = raw[g * SHIFTS : (g + 1) * SHIFTS] * (scale[c] * gain)
                if c == 0:
                    parts[base + g] = term
                else:
                    parts[base + g] += term

    def close(i, carry):
        trace_copy(i).wait_send()
        return carry

    def work(i, carry):
        source = flipped(me, i, blocks)

        @pl.when(i == 2)
        def _():
            lax.fori_loop(blocks // 2, first_wave, close, 0)
            lax.fori_loop(first_wave, blocks, post, 0)

        @pl.when(i > 0)
        def _():
            trace_copy(i).wait_recv()

        prepare(source)
        products(source)
        return carry

    lax.fori_loop(0, blocks, work, 0)

    piece = lags // LANES // 4
    own_side, far_side = lax.div(mine, 2), lax.div(far, 2)

    def some(j):
        return pl.ds(bounds[j], bounds[j + 1] - bounds[j])

    def spots(number):
        return pl.ds(pl.multiple_of(number * piece, 8), piece)

    def near_copy(j, side):
        number = lax.rem(near, 2) + 2 * side
        return pltpu.make_async_remote_copy(
            src_ref=turned.at[some(j), spots(number)],
            dst_ref=near_recv.at[side, some(j)],
            send_sem=near_send_sem.at[j, side],
            recv_sem=near_recv_sem.at[j, side],
            device_id={"ch": near},
            device_id_type=MESH,
        )

    def far_copy(j):
        return pltpu.make_async_remote_copy(
            src_ref=far_send.at[some(j)],
            dst_ref=far_recv.at[some(j)],
            send_sem=far_send_sem.at[j],
            recv_sem=far_recv_sem.at[j],
            device_id={"ch": far},
            device_id_type=MESH,
        )

    def peaks_copy(j):
        return pltpu.make_async_remote_copy(
            src_ref=peaks_send.at[j],
            dst_ref=peaks_recv.at[j],
            send_sem=peaks_send_sem.at[j],
            recv_sem=peaks_recv_sem.at[j],
            device_id={"ch": far},
            device_id_type=MESH,
        )

    def turn(j, carry):
        both = []
        for i in range(2):
            k = 2 * j + i
            both.append(
                parts[entry(2 * LANES + k, blocks * slots - 1)]
                + parts[entry(2 * LANES + HALVES + k, blocks * slots - 1)]
            )
        stack = []
        for t in range(TURNS // 2):
            a, b = (x[:, t * LANES : (t + 1) * LANES] for x in both)
            stack.append(jnp.where(low, a, pltpu.roll(b, LANES // 2, 1)))
            stack.append(jnp.where(low, pltpu.roll(a, LANES // 2, 1), b))
        flat = jnp.concatenate(stack, axis=0).T
        for i in range(2):
            for b in range(STEP):
                at = (i * STEP + b) * SHIFTS
                turned[2 * j + i, pl.ds(b, SHIFTS, stride=STEP), :] = flat[at : at + SHIFTS]
        return carry

    def pass_on(j):
        near_copy(j, far_side).wait_recv()
        value = turned[some(j), spots(far)] + near_recv[far_side, some(j)]
        tiles = value.reshape(-1, 8, LANES)
        peak = jnp.maximum(jnp.max(jnp.abs(tiles), axis=0), TINY)
        peaks_send[j] = peak
        peaks_copy(j).start()
        whole = jnp.round(tiles * (MOST / peak)[None]).astype(jnp.int32)
        far_send[some(j)] = whole.reshape(value.shape).astype(jnp.int16)
        far_copy(j).start()

    def lay(target, j, value):
        first, count = bounds[j], bounds[j + 1] - bounds[j]
        summed[: count * piece, :] = value.reshape(count * piece, LANES)
        for k in range(0, count, 8):
            size = min(8, count - k)
            for r in range(piece):
                found = summed[pl.ds(k * piece + r, size, stride=piece), :]
                target[first + k : first + k + size, r * LANES : (r + 1) * LANES] = found

    pieces = len(bounds) - 1
    for j in range(pieces):
        lax.fori_loop(bounds[j] // 2, bounds[j + 1] // 2, turn, 0, unroll=4)
        near_copy(j, far_side).start()
        if j > 0:
            pass_on(j - 1)
            near_copy(j - 1, own_side).start()
    pass_on(pieces - 1)
    near_copy(pieces - 1, own_side).start()
    for j in range(pieces):
        near_copy(j, own_side).wait_recv()
        lay(near_ref, j, turned[some(j), spots(mine)] + near_recv[own_side, some(j)])
    for j in range(pieces):
        peaks_copy(j).wait_recv()
        far_copy(j).wait_recv()
        whole = far_recv[some(j)].astype(jnp.int32).astype(F32)
        tiles = whole.reshape(-1, 8, LANES) * (peaks_recv[j] * (1.0 / MOST))[None]
        lay(far_ref, j, tiles)
    for j in range(pieces):
        near_copy(j, far_side).wait_send()
        near_copy(j, own_side).wait_send()
        far_copy(j).wait_send()
        peaks_copy(j).wait_send()

    lax.fori_loop(1, blocks // 2, close, 0)
    lax.fori_loop(first_wave, blocks, close, 0)


def per_device(waveform, templates, block_of, trace_of):
    me = lax.axis_index("st")
    blocks = lax.axis_size("st")
    own, chans, taps = templates.shape
    half = chans // 2
    stations, comps, window = waveform.shape
    lags = window - taps
    used = window // LANES
    depth = taps + LANES
    pairs = 2 * own
    slots = -(-13 * pairs // (10 * blocks))
    bounds = (0, 8, 24, 40, own)
    count = len(bounds) - 1
    assert 40 < own <= HALVES and own % 4 == 0 and lags == 64 * LANES and used % 4 == 0

    wave = jnp.transpose(waveform, (1, 0, 2))
    traces = jnp.transpose(trace_of[0], (0, 2, 1))
    named = jnp.transpose(block_of[0], (1, 0))

    spots = np.arange(LANES)
    later = spots[:, None] >= spots[None, :]
    steps = np.concatenate([later, ~later, np.ones_like(later)], axis=1)
    steps = jnp.asarray(np.concatenate([steps, steps], axis=0), BF16)

    dims = (blocks, slots, own, half, taps, used, depth, lags, bounds)
    rows = half * used
    piece = lags // LANES // 4
    smem = pl.BlockSpec(memory_space=pltpu.SMEM)
    vmem = pl.BlockSpec(memory_space=pltpu.VMEM)
    dma = pltpu.SemaphoreType.DMA
    given = (traces, named, wave, templates, steps)
    given = [pltpu.with_memory_space_constraint(x, pltpu.HBM) for x in given]
    near, far = pl.pallas_call(
        functools.partial(kernel, dims),
        out_shape=[pltpu.VMEM((own, piece * LANES), F32)] * 2,
        in_specs=[pl.BlockSpec(memory_space=pltpu.HBM)] * 5,
        out_specs=[vmem, vmem],
        scratch_shapes=[
            pltpu.VMEM(traces.shape, jnp.int32),
            pltpu.VMEM(named.shape, jnp.int32),
            pltpu.VMEM(wave.shape, BF16),
            pltpu.VMEM(templates.shape, BF16),
            pltpu.VMEM(steps.shape, BF16),
            pltpu.VMEM((blocks * half, stations * comps), F32),
            pltpu.VMEM((8, 3 * LANES), jnp.int32),
            pltpu.SMEM((8, 3 * LANES), jnp.int32),
            pltpu.VMEM((blocks * rows, LANES), F32),
            pltpu.VMEM((blocks, rows, LANES), BF16),
            pltpu.VMEM((blocks, rows, LANES), BF16),
            pltpu.VMEM((2 * HALVES, half, SHIFTS, depth), BF16),
            pltpu.VMEM((2 * HALVES, half, LANES), F32),
            pltpu.VMEM((rows + 8, LANES), F32),
            pltpu.VMEM((TURNS - 1, rows + 8, LANES), F32),
            pltpu.VMEM((rows, LANES), F32),
            pltpu.VMEM((rows, LANES), F32),
            pltpu.VMEM((rows, LANES), F32),
            pltpu.VMEM((half, TURNS * TURNS, SHIFTS, LANES), BF16),
            pltpu.VMEM((half, SHIFTS, lags // SHIFTS), F32),
            pltpu.VMEM((blocks * slots, SHIFTS, lags // SHIFTS), F32),
            pltpu.VMEM((own, lags // LANES, LANES), F32),
            pltpu.VMEM((2, own, piece, LANES), F32),
            pltpu.VMEM((own, piece, LANES), jnp.int16),
            pltpu.VMEM((own, piece, LANES), jnp.int16),
            pltpu.VMEM((count, 8, LANES), F32),
            pltpu.VMEM((count, 8, LANES), F32),
            pltpu.VMEM((16 * piece, LANES), F32),
            dma((8,)),
            dma,
            dma((count,)),
            dma((count,)),
            dma((blocks,)),
            dma((blocks,)),
            dma((count, 2)),
            dma((count, 2)),
            dma((count,)),
            dma((count,)),
        ],
        compiler_params=pltpu.CompilerParams(
            collective_id=0, has_side_effects=True, vmem_limit_bytes=(52 + blocks) * 512 * 1024
        ),
        name="detect",
    )(*given)
    return near + far


def solution(mesh):
    in_specs = (
        P("st", None, None),
        P("st", "ch", None),
        P("ch", None, None),
        P("ch", None, None, None),
    )
    return jax.shard_map(
        per_device, mesh=mesh, in_specs=in_specs, out_specs=P("st", "ch"), check_vma=False
    )
```
